768 devices in a mesh: row: 96 (over x, z, core), grp: 8 (over y).
Axes of the slice: x: 4, y: 8, z: 12, core: 2. Of those that a mesh axis runs over, the one named last changes fastest.
Arguments:
- source: bfloat16 [98304, 256], P(('row', 'grp')), may hold values from -0.5 to 0.5
- target: bfloat16 [98304, 256], P(('row', 'grp')), may hold values from -0.5 to 0.5
- pair_mask: int32 [96, 5], P('row'), may hold values from 0 to 1, as said below
Outputs:
- source_grad: float32 [98304, 256], P(('row', 'grp'))
- target_grad: float32 [98304, 256], P(('row', 'grp'))
The draws below stay inside these ranges and needn't reach their ends.
Inputs may be any that keep to these rules, and one draw needn't show every extreme that they name: pair_mask[b, 2] = 1 for every block b: each source block is paired with the target block of the same index.
All inputs are finite; a program needn't handle non-finite values.
Results may differ from the reference program's by a relative error of at most 0.0035.
Values may be sent and summed in bfloat16 or wider, within the bound.
No kernel may reach another device: no remote copies, remote signals or barrier semaphores. Data moves between devices by JAX's collectives and lax.ppermute only.
A program may use at most 32 MiB of HBM per device.

```python
import math
import jax
import jax.numpy as jnp
from jax import lax

E = 256
BLK = 1024
HALF = 2
ITERS = 3
WIN = 5
NB = 96
ROWS = 98304


def normal_rows(key):
    spread = 2.0 / math.sqrt(E)
    values = jax.random.normal(key, (ROWS, E), jnp.float32)
    return jnp.clip(values, -4.0, 4.0) * spread


def draw_source(key, part):
    key = jax.random.fold_in(key, 11)
    return normal_rows(key).astype(jnp.bfloat16)


def draw_target(key, part):
    key = jax.random.fold_in(key, 12)
    return normal_rows(key).astype(jnp.bfloat16)


def draw_pair_mask(key, part):
    key = jax.random.fold_in(key, 13)
    first_key, second_key = jax.random.split(key)
    levels = jax.random.randint(first_key, (NB, 1), 0, 5)
    rolls = jax.random.randint(second_key, (NB, WIN), 0, 4)
    chosen = (rolls < levels).astype(jnp.int32)
    middle = (jnp.arange(WIN) == WIN // 2)[None, :]
    return jnp.where(middle, 1, chosen).astype(jnp.int32)


def setup_inputs(seed: int = 0) -> dict:
    seeds = jax.random.split(jax.random.key(seed), 4)
    source = draw_source(jax.random.fold_in(seeds[3], 71), 0)
    target = draw_target(jax.random.fold_in(seeds[3], 71), 0)
    pair_mask = draw_pair_mask(jax.random.fold_in(seeds[3], 71), 0)
    return dict(source=source, target=target, pair_mask=pair_mask)


EPS = 0.1
NEG = -1.0e30


def reference(source, target, pair_mask):
    source_blocks = source.reshape(NB, BLK, E)
    target_blocks = target.reshape(NB, BLK, E)
    slot_ids = jnp.arange(WIN, dtype=jnp.int32)
    block_ids = jnp.arange(NB, dtype=jnp.int32)
    target_ids = (block_ids[:, None] + slot_ids[None, :] - HALF) % NB
    owner_ids = (block_ids[:, None] - slot_ids[None, :] + HALF) % NB
    listed = pair_mask == 1
    source_norms = jnp.sum(jnp.square(source_blocks.astype(jnp.float32)), axis=2)
    target_norms = jnp.sum(jnp.square(target_blocks.astype(jnp.float32)), axis=2)

    def block_cost(owner):
        rows_here = source_blocks[owner]

        def one_pair(other):
            inner = jnp.dot(rows_here, target_blocks[other].T, preferred_element_type=jnp.float32)
            return source_norms[owner][:, None] + target_norms[other][None, :] - 2.0 * inner

        return lax.map(one_pair, target_ids[owner])

    cost_tiles = lax.map(block_cost, block_ids)
    potentials = jnp.zeros((NB, BLK), jnp.float32)
    duals = jnp.zeros((NB, BLK), jnp.float32)

    def row_pass(inputs):
        tiles, window_pot, keep_rows = inputs
        scores = jnp.where(keep_rows[:, None, None], (window_pot[:, None, :] - tiles) / EPS, NEG)
        peak_vals = jnp.max(scores, axis=(0, 2))
        sums_here = jnp.sum(jnp.exp(scores - peak_vals[None, :, None]), axis=(0, 2))
        return -EPS * (peak_vals + jnp.log(sums_here))

    def col_pass(inputs):
        tiles, duals_here, keep_rows = inputs
        scores = jnp.where(keep_rows[:, None, None], (duals_here[None, :, None] - tiles) / EPS, NEG)
        peak_vals = jnp.max(scores, axis=1)
        sums_here = jnp.sum(jnp.exp(scores - peak_vals[:, None, :]), axis=1)
        return peak_vals, sums_here

    for repeat_index in range(ITERS):
        window_pot = potentials[target_ids]
        duals = lax.map(row_pass, (cost_tiles, window_pot, listed))
        col_peak, col_sums = lax.map(col_pass, (cost_tiles, duals, listed))
        gathered_peak = col_peak[owner_ids, slot_ids[None, :]]
        gathered_sums = col_sums[owner_ids, slot_ids[None, :]]
        best_peak = jnp.max(gathered_peak, axis=1)
        weighted = jnp.sum(gathered_sums * jnp.exp(gathered_peak - best_peak[:, None, :]), axis=1)
        potentials = -EPS * (best_peak + jnp.log(weighted))

    window_pot = potentials[target_ids]

    def grad_pass(inputs):
        tiles, duals_here, pot_here, keep_rows, rows_here, other_ids = inputs
        window_rows = target_blocks[other_ids].astype(jnp.float32)
        transport_plan = jnp.where(keep_rows[:, None, None],
                              jnp.exp(((duals_here[None, :, None] + pot_here[:, None, :]) - tiles) / EPS),
                              0.0).astype(jnp.bfloat16)
        weights = transport_plan.astype(jnp.float32)
        row_mass = jnp.sum(weights, axis=(0, 2))
        carried_along = jnp.einsum('dij,dje->ie', weights, window_rows)
        grad_rows = 2.0 * (rows_here.astype(jnp.float32) * row_mass[:, None] - carried_along)
        col_mass = jnp.sum(weights, axis=1)
        pulled_values = jnp.einsum('dij,ie->dje', weights, rows_here.astype(jnp.float32))
        partials = window_rows * col_mass[:, :, None] - pulled_values
        return grad_rows, partials

    grad_rows, partials = lax.map(grad_pass, (cost_tiles, duals, window_pot, listed, source_blocks, target_ids))
    target_sum = jnp.sum(partials[owner_ids, slot_ids[None, :]], axis=1)
    return grad_rows.reshape(ROWS, E), (2.0 * target_sum).reshape(ROWS, E)
```

```python
import functools
import math

import jax
import jax.numpy as jnp
from jax import lax
from jax.experimental import pallas as pl
from jax.experimental.pallas import tpu as pltpu
from jax.sharding import PartitionSpec as P

ITERS = 3
EPS = 0.1
NEG = -1e30
KAPPA = 1.0 / (EPS * math.log(2.0))
TWO_KAPPA = 2.0 * KAPPA
SAFE_SUM = 2.0 ** -60
LANES = 128
WINDOW = 5


def from_row(block, source_of):
    count = lax.axis_size("row")
    return lax.ppermute(block, "row", [(source_of(i), i) for i in range(count)])


def swap_mate(block):
    return from_row(block, lambda i: i ^ 1)


def shifted(block, distance):
    count = lax.axis_size("row")
    return from_row(block, lambda i: (i - distance) % count)


def from_chip(block, reach):
    count = lax.axis_size("row")

    def source_of(i):
        step = -2 * reach if i % 2 == 0 else 2 * reach
        return (i + step) % count

    return from_row(block, source_of)


def swap_cross(block):
    count = lax.axis_size("row")
    return from_row(block, lambda i: (i - 1 if i % 2 == 0 else i + 1) % count)


def gathered(shard):
    count = lax.axis_size("grp")
    copies = jnp.broadcast_to(shard[None], (count,) + shard.shape)
    return lax.all_to_all(copies, "grp", 0, 0, tiled=True).reshape(-1, shard.shape[1])


def lse2(a, b):
    top = jnp.maximum(a, b)
    return top + jnp.log2(jnp.exp2(a - top) + jnp.exp2(b - top))


def column_totals(partial, even):
    own, mate, cross, up, down = (partial[p] for p in range(WINDOW))
    none = jnp.full_like(own, NEG)
    six = jnp.where(
        even,
        jnp.stack([down, cross, own, mate, up, none]),
        jnp.stack([none, down, mate, own, cross, up]),
    )
    chip = lse2(six, swap_mate(six))
    near = from_chip(jnp.where(even, chip[2:6], chip[0:4]), 1)
    far = from_chip(jnp.where(even, chip[4:6], chip[0:2]), 2)
    blank = jnp.full_like(far, NEG)
    outer = jnp.where(
        even,
        jnp.concatenate([lse2(near[0:2], far), near[2:4], blank]),
        jnp.concatenate([blank, near[0:2], lse2(near[2:4], far)]),
    )
    total = lse2(chip, lse2(outer, swap_mate(outer)))
    return jnp.where(
        even,
        jnp.stack([total[2], total[3], total[1], total[4], total[0]]),
        jnp.stack([total[3], total[2], total[4], total[5], total[1]]),
    )


def dot_nt(a, b):
    return lax.dot_general(a, b, (((1,), (1,)), ((), ())), preferred_element_type=jnp.float32)


def step_kernel(first, listed, pot, rows, t0, t1, t2, t3, t4, sums_out, dual_out, bias, scores, peak, col):
    targets = (t0, t1, t2, t3, t4)
    count = rows.shape[0]
    tile = min(256, count)
    for p in range(WINDOW):
        if first:
            sq = jnp.square(targets[p][...].astype(jnp.float32))
            high = sq.astype(jnp.bfloat16)
            low = (sq - high.astype(jnp.float32)).astype(jnp.bfloat16)
            ones = jnp.ones((8, sq.shape[1]), jnp.bfloat16)
            row = -KAPPA * (dot_nt(ones, high) + dot_nt(ones, low))[0:1]
        else:
            row = pot[p : p + 1, :]
        bias[p : p + 1, :] = jnp.where(listed[p] == 1, row, NEG)

    peak[...] = jnp.full(peak.shape, NEG, jnp.float32)
    for p in range(WINDOW):

        def fill(c, carry, p=p):
            at = pl.multiple_of(c * tile, tile)
            inner = dot_nt(rows[...], targets[p][pl.ds(at, tile), :])
            block = inner * TWO_KAPPA + bias[p : p + 1, pl.ds(at, tile)]
            scores[:, pl.ds(pl.multiple_of(p * count + at, tile), tile)] = block
            best = peak[...]
            for q in range(tile // LANES):
                best = jnp.maximum(best, block[:, q * LANES : (q + 1) * LANES])
            peak[...] = best
            return carry

        lax.fori_loop(0, count // tile, fill, 0)

    col[...] = jnp.zeros(col.shape, jnp.float32)
    width = WINDOW * count // LANES

    def chunk(r, carry):
        here = pl.ds(pl.multiple_of(r * LANES, LANES), LANES)
        top = jnp.max(peak[here, :], axis=1, keepdims=True)
        acc = jnp.zeros((LANES, LANES), jnp.float32)
        for q in range(width):
            e = jnp.exp2(scores[here, q * LANES : (q + 1) * LANES] - top)
            scores[here, q * LANES : (q + 1) * LANES] = e
            acc = acc + e
        total = jnp.sum(acc, axis=1, keepdims=True)
        dual_out[here, :] = jnp.broadcast_to(-(top + jnp.log2(total)), (LANES, LANES))
        scale = jnp.broadcast_to(1.0 / total, (LANES, LANES))
        for q in range(width):
            e = scores[here, q * LANES : (q + 1) * LANES] * scale
            col[:, q * LANES : (q + 1) * LANES] += jnp.sum(e.reshape(LANES // 8, 8, LANES), axis=0)
        return carry

    lax.fori_loop(0, count // LANES, chunk, 0)

    sums_out[...] = jnp.full(sums_out.shape, NEG, jnp.float32)
    for p in range(WINDOW):
        total = jnp.sum(col[:, p * count : (p + 1) * count], axis=0, keepdims=True)
        safe = jnp.min(total) >= SAFE_SUM
        usable = listed[p] == 1

        @pl.when(jnp.logical_and(usable, safe))
        def _(p=p, total=total):
            sums_out[p : p + 1, :] = jnp.log2(total) - bias[p : p + 1, :]

        @pl.when(jnp.logical_and(usable, jnp.logical_not(safe)))
        def _(p=p):
            def value(r):
                here = pl.ds(pl.multiple_of(r * LANES, LANES), LANES)
                return dot_nt(rows[here, :], targets[p][...]) * TWO_KAPPA + dual_out[here, 0:1]

            def find(r, best):
                return jnp.maximum(best, jnp.max(value(r), axis=0, keepdims=True))

            best = lax.fori_loop(0, count // LANES, find, jnp.full((1, count), NEG, jnp.float32))

            def add(r, acc):
                return acc + jnp.sum(jnp.exp2(value(r) - best), axis=0, keepdims=True)

            acc = lax.fori_loop(0, count // LANES, add, jnp.zeros((1, count), jnp.float32))
            sums_out[p : p + 1, :] = best + jnp.log2(acc)


def step(first, listed, pot, rows, targets):
    count, width = rows.shape
    vmem = pl.BlockSpec(memory_space=pltpu.VMEM)
    pairs = WINDOW * count * count
    return pl.pallas_call(
        functools.partial(step_kernel, first),
        out_shape=(
            jax.ShapeDtypeStruct((8, count), jnp.float32),
            jax.ShapeDtypeStruct((count, LANES), jnp.float32),
        ),
        in_specs=[pl.BlockSpec(memory_space=pltpu.SMEM)] + [vmem] * 7,
        out_specs=(vmem, vmem),
        scratch_shapes=[
            pltpu.VMEM((8, count), jnp.float32),
            pltpu.VMEM((count, WINDOW * count), jnp.float32),
            pltpu.VMEM((count, LANES), jnp.float32),
            pltpu.VMEM((8, WINDOW * count), jnp.float32),
        ],
        compiler_params=pltpu.CompilerParams(vmem_limit_bytes=44 * 1024 * 1024),
        cost_estimate=pl.CostEstimate(
            flops=2 * pairs * width, bytes_accessed=12 * count * width, transcendentals=pairs
        ),
        name="sinkhorn_step",
    )(listed, pot, rows, *targets)


def grad_kernel(scal, pot, dual, mine, rows, t0, t1, t2, t3, t4, source_out, o0, o1, o2, o3, o4):
    targets = (t0, t1, t2, t3, t4)
    outs = (o0, o1, o2, o3, o4)
    count = rows.shape[0]
    at = pl.multiple_of(scal[WINDOW] * LANES, LANES)
    here = pl.ds(at, LANES)
    own_dual = dual[here, 0:1]
    dual_row = jnp.concatenate(
        [dual[r * LANES : (r + 1) * LANES, :].T[0:1, :] for r in range(count // LANES)], axis=1
    )
    mass = jnp.zeros((LANES, 1), jnp.float32)
    carried = jnp.zeros((LANES, rows.shape[1]), jnp.float32)
    for p in range(WINDOW):
        bias = jnp.where(scal[p] == 1, pot[p : p + 1, :], NEG)
        weight = jnp.exp2(dot_nt(mine[...], targets[p][...]) * TWO_KAPPA + (own_dual + bias))
        weight = weight.astype(jnp.bfloat16)
        mass = mass + jnp.sum(weight.astype(jnp.float32), axis=1, keepdims=True)
        carried = carried + jnp.dot(weight, targets[p][...], preferred_element_type=jnp.float32)
    source_out[...] = 2.0 * (mine[...].astype(jnp.float32) * mass - carried)

    for p in range(WINDOW):
        bias = jnp.where(scal[p] == 1, pot[p : p + 1, here], NEG)
        bias = jnp.broadcast_to(bias, (LANES, LANES)).T[:, 0:1]
        some = targets[p][here, :]
        weight = jnp.exp2(dot_nt(some, rows[...]) * TWO_KAPPA + (dual_row + bias))
        weight = weight.astype(jnp.bfloat16)
        mass = jnp.sum(weight.astype(jnp.float32), axis=1, keepdims=True)
        pulled = jnp.dot(weight, rows[...], preferred_element_type=jnp.float32)
        outs[p][...] = some.astype(jnp.float32) * mass - pulled


def gradients(scal, pot, dual, mine, rows, targets):
    count, width = rows.shape
    vmem = pl.BlockSpec(memory_space=pltpu.VMEM)
    part = jax.ShapeDtypeStruct((LANES, width), jnp.float32)
    pairs = 2 * WINDOW * count * LANES
    return pl.pallas_call(
        grad_kernel,
        out_shape=(part,) * (1 + WINDOW),
        in_specs=[pl.BlockSpec(memory_space=pltpu.SMEM)] + [vmem] * 9,
        out_specs=(vmem,) * (1 + WINDOW),
        compiler_params=pltpu.CompilerParams(vmem_limit_bytes=44 * 1024 * 1024),
        cost_estimate=pl.CostEstimate(
            flops=4 * pairs * width, bytes_accessed=16 * count * width, transcendentals=pairs
        ),
        name="plan_gradients",
    )(scal, pot, dual, mine, rows, *targets)


def shards(source, target, pair_mask):
    even = lax.axis_index("row") % 2 == 0
    own = gathered(target)
    above = shifted(own, -2)
    below = shifted(own, 2)
    mate = swap_mate(own)
    cross = swap_mate(jnp.where(even, above, below))
    rows = gathered(source)
    targets = (own, mate, cross, above, below)
    mask = pair_mask[0]
    listed = jnp.where(even, mask[jnp.array([2, 3, 1, 4, 0])], mask[jnp.array([2, 1, 3, 4, 0])])
    pot = jnp.zeros((WINDOW, own.shape[0]), jnp.float32)
    dual = None
    for k in range(ITERS):
        partial, dual = step(k == 0, listed, pot, rows, targets)
        pot = -column_totals(partial, even)
    scal = jnp.concatenate([listed, lax.axis_index("grp").astype(jnp.int32)[None]])
    source_grad, part_own, part_mate, part_cross, part_above, part_below = gradients(
        scal, pot, dual, source, rows, targets
    )
    total = (
        part_own
        + swap_mate(part_mate)
        + swap_cross(part_cross)
        + shifted(part_above, 2)
        + shifted(part_below, -2)
    )
    return source_grad, 2.0 * total


def solution(mesh):
    placed = (P(("row", "grp"), None), P(("row", "grp"), None), P("row", None))
    return jax.shard_map(
        shards,
        mesh=mesh,
        in_specs=placed,
        out_specs=(P(("row", "grp"), None), P(("row", "grp"), None)),
        check_vma=False,
    )
```

```python
import functools
import math

import jax
import jax.numpy as jnp
from jax import lax
from jax.experimental import pallas as pl
from jax.experimental.pallas import tpu as pltpu
from jax.sharding import PartitionSpec as P

ITERS = 3
EPS = 0.1
NEG = -1e30
KAPPA = 1.0 / (EPS * math.log(2.0))
TWO_KAPPA = 2.0 * KAPPA
SAFE_SUM = 2.0 ** -60
SAFE_ROW = 2.0 ** -28
SAFE_SHIFT = 60.0
SCOPED = 16 * 1024 * 1024
LANES = 128
WINDOW = 5


def from_row(block, source_of):
    count = lax.axis_size("row")
    return lax.ppermute(block, "row", [(source_of(i), i) for i in range(count)])


def swap_mate(block):
    return from_row(block, lambda i: i ^ 1)


def shifted(block, distance):
    count = lax.axis_size("row")
    return from_row(block, lambda i: (i - distance) % count)


def from_chip(block, reach):
    count = lax.axis_size("row")

    def source_of(i):
        step = -2 * reach if i % 2 == 0 else 2 * reach
        return (i + step) % count

    return from_row(block, source_of)


def swap_cross(block):
    count = lax.axis_size("row")
    return from_row(block, lambda i: (i - 1 if i % 2 == 0 else i + 1) % count)


def gathered(shard):
    count = lax.axis_size("grp")
    copies = jnp.broadcast_to(shard[None], (count,) + shard.shape)
    return lax.all_to_all(copies, "grp", 0, 0, tiled=True).reshape(-1, shard.shape[1])


def lse2(a, b):
    top = jnp.maximum(a, b)
    return top + jnp.log2(jnp.exp2(a - top) + jnp.exp2(b - top))


def column_totals(partial, even):
    own, mate, cross, up, down = (partial[p] for p in range(WINDOW))
    none = jnp.full_like(own, NEG)
    six = jnp.where(
        even,
        jnp.stack([down, cross, own, mate, up, none]),
        jnp.stack([none, down, mate, own, cross, up]),
    )
    chip = lse2(six, swap_mate(six))
    near = from_chip(jnp.where(even, chip[2:6], chip[0:4]), 1)
    far = from_chip(jnp.where(even, chip[4:6], chip[0:2]), 2)
    blank = jnp.full_like(far, NEG)
    outer = jnp.where(
        even,
        jnp.concatenate([lse2(near[0:2], far), near[2:4], blank]),
        jnp.concatenate([blank, near[0:2], lse2(near[2:4], far)]),
    )
    total = lse2(chip, lse2(outer, swap_mate(outer)))
    return jnp.where(
        even,
        jnp.stack([total[2], total[3], total[1], total[4], total[0]]),
        jnp.stack([total[3], total[2], total[4], total[5], total[1]]),
    )


def dot_nt(a, b):
    return lax.dot_general(a, b, (((1,), (1,)), ((), ())), preferred_element_type=jnp.float32)


def exact_columns(rows, target, dual):
    count = rows.shape[0]

    def value(r):
        here = pl.ds(pl.multiple_of(r * LANES, LANES), LANES)
        return dot_nt(rows[here, :], target[...]) * TWO_KAPPA + dual[here, 0:1]

    def find(r, best):
        return jnp.maximum(best, jnp.max(value(r), axis=0, keepdims=True))

    best = lax.fori_loop(0, count // LANES, find, jnp.full((1, count), NEG, jnp.float32))

    def add(r, acc):
        return acc + jnp.sum(jnp.exp2(value(r) - best), axis=0, keepdims=True)

    acc = lax.fori_loop(0, count // LANES, add, jnp.zeros((1, count), jnp.float32))
    return best + jnp.log2(acc)


def put_columns(listed, base, col, sums_out, fine):
    count = sums_out.shape[1]
    sums_out[...] = jnp.full(sums_out.shape, NEG, jnp.float32)
    for p in range(WINDOW):
        sums = jnp.sum(col[:, p * count : (p + 1) * count], axis=0, keepdims=True)
        taken = listed[p] == 1
        sums_out[p : p + 1, :] = jnp.where(taken, jnp.log2(sums) - base[p : p + 1, :], NEG)
        good = jnp.where(jnp.logical_or(jnp.logical_not(taken), sums >= SAFE_SUM), 1.0, 0.0)
        for q in range(count // LANES):
            fine = jnp.minimum(fine, good[:, q * LANES : (q + 1) * LANES])
    return jnp.min(fine) > 0.5


def put_exact_columns(listed, fetch, dual, sums_out):
    for p in range(WINDOW):

        @pl.when(listed[p] == 1)
        def _(p=p):
            sums_out[p : p + 1, :] = exact_columns(*fetch(p), dual)


def add_columns(entries, here, scale, col, width):
    for q in range(width):
        e = entries[here, q * LANES : (q + 1) * LANES] * scale
        col[:, q * LANES : (q + 1) * LANES] += jnp.sum(e.reshape(LANES // 8, 8, LANES), axis=0)


def first_kernel(listed, rows, t0, t1, t2, t3, t4, entries, sums_out, top_out, base, dual, peak, col):
    targets = (t0, t1, t2, t3, t4)
    count = rows.shape[0]
    base[...] = jnp.zeros(base.shape, jnp.float32)
    peak[...] = jnp.full(peak.shape, NEG, jnp.float32)
    for p in range(WINDOW):
        sq = jnp.square(targets[p][...].astype(jnp.float32))
        sq = sum(sq[:, q * LANES : (q + 1) * LANES] for q in range(sq.shape[1] // LANES))
        bias = jnp.concatenate(
            [
                jnp.sum(sq[r * LANES : (r + 1) * LANES, :].T, axis=0, keepdims=True)
                for r in range(count // LANES)
            ],
            axis=1,
        )
        bias = -KAPPA * bias
        bias = jnp.where(listed[p] == 1, bias, NEG)
        base[p : p + 1, :] = bias

        block = dot_nt(rows[...], targets[p][...]) * TWO_KAPPA + bias
        entries[:, p * count : (p + 1) * count] = block
        best = peak[...]
        for q in range(count // LANES):
            best = jnp.maximum(best, block[:, q * LANES : (q + 1) * LANES])
        peak[...] = best

    col[...] = jnp.zeros(col.shape, jnp.float32)
    width = WINDOW * count // LANES

    def rows_of(r):
        return pl.ds(pl.multiple_of(r * LANES, LANES), LANES)

    def exponentials(r, meanwhile):
        here = rows_of(r)
        top = jnp.broadcast_to(jnp.max(peak[here, :], axis=1, keepdims=True), (LANES, LANES))
        acc = jnp.zeros((LANES, LANES), jnp.float32)
        for q in range(width):
            e = jnp.exp2(entries[here, q * LANES : (q + 1) * LANES] - top)
            entries[here, q * LANES : (q + 1) * LANES] = e
            acc = acc + e
        total = jnp.broadcast_to(jnp.sum(acc, axis=1, keepdims=True), (LANES, LANES))
        meanwhile()
        top_out[here, :] = top
        dual[here, :] = -(top + jnp.log2(total))
        peak[here, :] = 1.0 / total

    def columns(r):
        add_columns(entries, rows_of(r), peak[rows_of(r), :], col, width)

    def both(r, carry):
        exponentials(r, lambda: columns(r - 1))
        return carry

    exponentials(0, lambda: None)
    lax.fori_loop(1, count // LANES, both, 0)
    columns(count // LANES - 1)
    fine = put_columns(listed, base, col, sums_out, jnp.ones((1, LANES), jnp.float32))

    @pl.when(jnp.logical_not(fine))
    def _():
        put_exact_columns(listed, lambda p: (rows, targets[p]), dual, sums_out)


def later_kernel(
    listed, entries, pot, base, top, rows_far, t0, t1, t2, t3, t4, sums_out, dual_out, gain, col, low, total, rows, target
):
    targets = (t0, t1, t2, t3, t4)
    count = rows.shape[0]

    def fetch(p):
        pltpu.sync_copy(rows_far, rows)
        pltpu.sync_copy(targets[p], target)
        return rows, target

    col[...] = jnp.zeros(col.shape, jnp.float32)
    width = WINDOW * count // LANES
    worst = jnp.zeros((1, count), jnp.float32)
    for p in range(WINDOW):
        taken = listed[p] == 1
        shift = jnp.where(taken, pot[p : p + 1, :] - base[p : p + 1, :], 0.0)
        worst = jnp.maximum(worst, jnp.abs(shift))
        gain[:, p * count : (p + 1) * count] = jnp.broadcast_to(
            jnp.where(taken, jnp.exp2(shift), 0.0), (8, count)
        )
    low[...] = jnp.full(low.shape, 1.0, jnp.float32)

    def rows_of(r):
        return pl.ds(pl.multiple_of(r * LANES, LANES), LANES)

    def weigh(r, meanwhile):
        here = rows_of(r)
        acc = jnp.zeros((LANES, LANES), jnp.float32)
        for q in range(width):
            at = slice(q * LANES, (q + 1) * LANES)
            acc = acc + entries[here, at] * gain[0:1, at]
        mass = jnp.broadcast_to(jnp.sum(acc, axis=1, keepdims=True), (LANES, LANES))
        meanwhile()
        low[...] = jnp.minimum(low[...], mass)
        dual_out[here, :] = -(top[here, :] + jnp.log2(mass))
        total[here, :] = 1.0 / mass

    def columns(r):
        add_columns(entries, rows_of(r), total[rows_of(r), :], col, width)

    def both(r, carry):
        weigh(r, lambda: columns(r - 1))
        return carry

    weigh(0, lambda: None)
    lax.fori_loop(1, count // LANES, both, 0)
    columns(count // LANES - 1)
    fine = jnp.where(jnp.min(low[...], axis=0, keepdims=True) >= SAFE_ROW, 1.0, 0.0)
    for q in range(count // LANES):
        fine = jnp.minimum(fine, jnp.where(worst[:, q * LANES : (q + 1) * LANES] <= SAFE_SHIFT, 1.0, 0.0))
    fine = put_columns(listed, base, col, sums_out, fine)

    @pl.when(jnp.logical_not(fine))
    def _():
        def value(p, here):
            bias = jnp.where(listed[p] == 1, pot[p : p + 1, :], NEG)
            return dot_nt(rows[here, :], target[...]) * TWO_KAPPA + bias

        dual_out[...] = jnp.full(dual_out.shape, NEG, jnp.float32)
        for p in range(WINDOW):
            fetch(p)

            def find(r, carry, p=p):
                here = pl.ds(pl.multiple_of(r * LANES, LANES), LANES)
                best = jnp.max(value(p, here), axis=1, keepdims=True)
                dual_out[here, :] = jnp.maximum(dual_out[here, :], best)
                return carry

            lax.fori_loop(0, count // LANES, find, 0)
        total[...] = jnp.zeros(total.shape, jnp.float32)
        for p in range(WINDOW):
            fetch(p)

            def add(r, carry, p=p):
                here = pl.ds(pl.multiple_of(r * LANES, LANES), LANES)
                e = jnp.exp2(value(p, here) - dual_out[here, 0:1])
                total[here, :] += jnp.sum(e, axis=1, keepdims=True)
                return carry

            lax.fori_loop(0, count // LANES, add, 0)
        dual_out[...] = -(dual_out[...] + jnp.log2(total[...]))

        put_exact_columns(listed, fetch, dual_out, sums_out)


VMEM = pl.BlockSpec(memory_space=pltpu.VMEM)
ANY = pl.BlockSpec(memory_space=pl.ANY)
SMEM = pl.BlockSpec(memory_space=pltpu.SMEM)


def first_step(listed, rows, targets):
    count, width = rows.shape
    pairs = WINDOW * count * count
    row = jax.ShapeDtypeStruct((8, count), jnp.float32)
    column = jax.ShapeDtypeStruct((count, LANES), jnp.float32)
    return pl.pallas_call(
        first_kernel,
        out_shape=(pltpu.VMEM((count, WINDOW * count), jnp.float32), row, column, row),
        in_specs=[SMEM] + [VMEM] * 6,
        out_specs=(VMEM,) * 4,
        scratch_shapes=[
            pltpu.VMEM((count, LANES), jnp.float32),
            pltpu.VMEM((count, LANES), jnp.float32),
            pltpu.VMEM((8, WINDOW * count), jnp.float32),
        ],
        compiler_params=pltpu.CompilerParams(vmem_limit_bytes=SCOPED),
        cost_estimate=pl.CostEstimate(
            flops=2 * pairs * width, bytes_accessed=12 * count * width, transcendentals=pairs
        ),
        name="first_step",
    )(listed, rows, *targets)


def later_step(listed, entries, pot, base, top, rows, targets):
    count, width = rows.shape
    pairs = WINDOW * count * count
    row = jax.ShapeDtypeStruct((8, count), jnp.float32)
    column = jax.ShapeDtypeStruct((count, LANES), jnp.float32)
    entries = pltpu.with_memory_space_constraint(entries, pltpu.VMEM)
    return pl.pallas_call(
        later_kernel,
        out_shape=(row, column),
        in_specs=[SMEM] + [VMEM] * 4 + [ANY] * 6,
        out_specs=(VMEM, VMEM),
        scratch_shapes=[
            pltpu.VMEM((8, WINDOW * count), jnp.float32),
            pltpu.VMEM((8, WINDOW * count), jnp.float32),
            pltpu.VMEM((LANES, LANES), jnp.float32),
            pltpu.VMEM((count, LANES), jnp.float32),
            pltpu.VMEM((count, width), jnp.bfloat16),
            pltpu.VMEM((count, width), jnp.bfloat16),
        ],
        compiler_params=pltpu.CompilerParams(vmem_limit_bytes=SCOPED),
        cost_estimate=pl.CostEstimate(
            flops=4 * pairs, bytes_accessed=12 * count * width, transcendentals=0
        ),
        name="later_step",
    )(listed, entries, pot, base, top, rows, *targets)


def grad_kernel(scal, pot, dual, mine, rows, t0, t1, t2, t3, t4, source_out, o0, o1, o2, o3, o4):
    targets = (t0, t1, t2, t3, t4)
    outs = (o0, o1, o2, o3, o4)
    count = rows.shape[0]
    at = pl.multiple_of(scal[WINDOW] * LANES, LANES)
    here = pl.ds(at, LANES)
    own_dual = dual[here, 0:1]
    dual_row = jnp.concatenate(
        [dual[r * LANES : (r + 1) * LANES, :].T[0:1, :] for r in range(count // LANES)], axis=1
    )
    mass = jnp.zeros((LANES, 1), jnp.float32)
    carried = jnp.zeros((LANES, rows.shape[1]), jnp.float32)
    for p in range(WINDOW):
        bias = jnp.where(scal[p] == 1, pot[p : p + 1, :], NEG)
        weight = jnp.exp2(dot_nt(mine[...], targets[p][...]) * TWO_KAPPA + (own_dual + bias))
        weight = weight.astype(jnp.bfloat16)
        mass = mass + jnp.sum(weight.astype(jnp.float32), axis=1, keepdims=True)
        carried = carried + jnp.dot(weight, targets[p][...], preferred_element_type=jnp.float32)
    source_out[...] = 2.0 * (mine[...].astype(jnp.float32) * mass - carried)

    for p in range(WINDOW):
        bias = jnp.where(scal[p] == 1, pot[p : p + 1, here], NEG)
        bias = jnp.broadcast_to(bias, (LANES, LANES)).T[:, 0:1]
        some = targets[p][here, :]
        weight = jnp.exp2(dot_nt(some, rows[...]) * TWO_KAPPA + (dual_row + bias))
        weight = weight.astype(jnp.bfloat16)
        mass = jnp.sum(weight.astype(jnp.float32), axis=1, keepdims=True)
        pulled = jnp.dot(weight, rows[...], preferred_element_type=jnp.float32)
        outs[p][...] = some.astype(jnp.float32) * mass - pulled


def gradients(scal, pot, dual, mine, rows, targets):
    count, width = rows.shape
    part = jax.ShapeDtypeStruct((LANES, width), jnp.float32)
    pairs = 2 * WINDOW * count * LANES
    return pl.pallas_call(
        grad_kernel,
        out_shape=(part,) * (1 + WINDOW),
        in_specs=[SMEM] + [VMEM] * 9,
        out_specs=(VMEM,) * (1 + WINDOW),
        compiler_params=pltpu.CompilerParams(vmem_limit_bytes=SCOPED),
        cost_estimate=pl.CostEstimate(
            flops=4 * pairs * width, bytes_accessed=16 * count * width, transcendentals=pairs
        ),
        name="plan_gradients",
    )(scal, pot, dual, mine, rows, *targets)


def shards(source, target, pair_mask):
    even = lax.axis_index("row") % 2 == 0
    own = gathered(target)
    above = shifted(own, -2)
    below = shifted(own, 2)
    mate = swap_mate(own)
    cross = swap_mate(jnp.where(even, above, below))
    rows = gathered(source)
    targets = (own, mate, cross, above, below)
    mask = pair_mask[0]
    listed = jnp.where(even, mask[jnp.array([2, 3, 1, 4, 0])], mask[jnp.array([2, 1, 3, 4, 0])])
    entries, partial, top, base = first_step(listed, rows, targets)
    pot = -column_totals(partial, even)
    for _ in range(ITERS - 1):
        partial, dual = later_step(listed, entries, pot, base, top, rows, targets)
        pot = -column_totals(partial, even)
    scal = jnp.concatenate([listed, lax.axis_index("grp").astype(jnp.int32)[None]])
    source_grad, part_own, part_mate, part_cross, part_above, part_below = gradients(
        scal, pot, dual, source, rows, targets
    )
    total = (
        part_own
        + swap_mate(part_mate)
        + swap_cross(part_cross)
        + shifted(part_above, 2)
        + shifted(part_below, -2)
    )
    return source_grad, 2.0 * total


def solution(mesh):
    placed = (P(("row", "grp"), None), P(("row", "grp"), None), P("row", None))
    return jax.shard_map(
        shards,
        mesh=mesh,
        in_specs=placed,
        out_specs=(P(("row", "grp"), None), P(("row", "grp"), None)),
        check_vma=False,
    )
```

```python
import functools
import math

import jax
import jax.numpy as jnp
from jax import lax
from jax.experimental import pallas as pl
from jax.experimental.pallas import tpu as pltpu
from jax.sharding import PartitionSpec as P

ITERS = 3
EPS = 0.1
NEG = -1e30
KAPPA = 1.0 / (EPS * math.log(2.0))
TWO_KAPPA = 2.0 * KAPPA
SAFE_SUM = 2.0 ** -60
SAFE_ROW = 2.0 ** -28
SAFE_SHIFT = 60.0
SCOPED = 16 * 1024 * 1024
LANES = 128
WINDOW = 5


def from_row(block, source_of):
    count = lax.axis_size("row")
    return lax.ppermute(block, "row", [(source_of(i), i) for i in range(count)])


def swap_mate(block):
    return from_row(block, lambda i: i ^ 1)


def shifted(block, distance):
    count = lax.axis_size("row")
    return from_row(block, lambda i: (i - distance) % count)


def swap_chips(block, second):
    count = lax.axis_size("row")

    def source_of(i):
        chip, core = divmod(i, 2)
        reach = 1 + core
        up = (chip // reach) % 2 == 0
        if second:
            up = not up
        return (i + 2 * reach if up else i - 2 * reach) % count

    return from_row(block, source_of)


def gathered(shard):
    count = lax.axis_size("grp")
    copies = jnp.broadcast_to(shard[None], (count,) + shard.shape)
    return lax.all_to_all(copies, "grp", 0, 0, tiled=True).reshape(-1, shard.shape[1])


def lse2(a, b):
    top = jnp.maximum(a, b)
    return top + jnp.log2(jnp.exp2(a - top) + jnp.exp2(b - top))


def column_totals(partial, row, extra=False):
    even = row % 2 == 0
    up = (row // 2) // (1 + row % 2) % 2 == 0
    count = 2 if extra else 0
    other = swap_mate(partial[: 6 + count])
    chip = lse2(partial[:6], other[:6])
    to_above, to_below = chip[2:6], chip[0:4]
    if count:
        mine = partial[6:8]
        here = jnp.where(
            even, jnp.concatenate([mine, other[6:]]), jnp.concatenate([other[6:], mine])
        )
        to_above = jnp.concatenate([to_above, here])
        to_below = jnp.concatenate([to_below, here])
    one = swap_chips(jnp.where(up, to_above, to_below), False)
    two = swap_chips(jnp.where(up, to_below, to_above), True)
    above = jnp.where(up, one, two)
    below = jnp.where(up, two, one)
    blank = jnp.full_like(above[0:2], NEG)
    outer = jnp.where(
        even,
        jnp.concatenate([below[0:2], lse2(below[2:4], above[0:2]), above[2:4]]),
        jnp.concatenate([below[2:4], blank, above[0:2]]),
    )
    sent = jnp.concatenate([outer, below[4:], above[4:]]) if count else outer
    got = swap_mate(sent)
    total = lse2(chip, lse2(outer, got[:6]))

    def placed(rows):
        return jnp.where(
            even,
            jnp.stack([rows[2], rows[3], rows[1], rows[4], rows[0]]),
            jnp.stack([rows[3], rows[2], rows[4], rows[5], rows[1]]),
        )

    if not count:
        return placed(total)
    near = jnp.where(even, sent[6:], got[6:])
    around = jnp.concatenate([near[:4], here, near[4:]]).reshape(6, count, -1)
    return placed(total), placed(around)


def dot_nt(a, b):
    return lax.dot_general(a, b, (((1,), (1,)), ((), ())), preferred_element_type=jnp.float32)


def exact_columns(rows, target, dual):
    count = rows.shape[0]

    def value(r):
        here = pl.ds(pl.multiple_of(r * LANES, LANES), LANES)
        return dot_nt(rows[here, :], target[...]) * TWO_KAPPA + dual[here, 0:1]

    def find(r, best):
        return jnp.maximum(best, jnp.max(value(r), axis=0, keepdims=True))

    best = lax.fori_loop(0, count // LANES, find, jnp.full((1, count), NEG, jnp.float32))

    def add(r, acc):
        return acc + jnp.sum(jnp.exp2(value(r) - best), axis=0, keepdims=True)

    acc = lax.fori_loop(0, count // LANES, add, jnp.zeros((1, count), jnp.float32))
    return best + jnp.log2(acc)


def is_even():
    return lax.rem(lax.axis_index("row"), 2) == 0


def place(p):
    low, high = ((2, 3), (3, 2), (1, 4), (4, 5), (0, 1))[p]
    return pl.ds(jnp.where(is_even(), low, high), 1)


def is_listed(mask, p):
    low, high = ((2, 2), (3, 1), (1, 3), (4, 4), (0, 0))[p]
    return mask[0, jnp.where(is_even(), low, high)] == 1


def put_columns(mask, base, col, sums_out, fine):
    count = sums_out.shape[1]
    sums_out[...] = jnp.full(sums_out.shape, NEG, jnp.float32)
    for p in range(WINDOW):
        sums = jnp.sum(col[:, p * count : (p + 1) * count], axis=0, keepdims=True)
        taken = is_listed(mask, p)
        sums_out[place(p), :] = jnp.where(taken, jnp.log2(sums) - base[p : p + 1, :], NEG)
        good = jnp.where(jnp.logical_or(jnp.logical_not(taken), sums >= SAFE_SUM), 1.0, 0.0)
        for q in range(count // LANES):
            fine = jnp.minimum(fine, good[:, q * LANES : (q + 1) * LANES])
    return jnp.min(fine) > 0.5


def put_exact_columns(mask, fetch, dual, sums_out):
    for p in range(WINDOW):

        @pl.when(is_listed(mask, p))
        def _(p=p):
            sums_out[place(p), :] = exact_columns(*fetch(p), dual)


def add_columns(entries, here, scale, col, width):
    for q in range(width):
        e = entries[here, q * LANES : (q + 1) * LANES] * scale
        col[:, q * LANES : (q + 1) * LANES] += jnp.sum(e.reshape(LANES // 8, 8, LANES), axis=0)


def first_kernel(mask, rows, t0, t1, t2, t3, t4, entries, sums_out, top_out, base, dual, peak, col):
    targets = (t0, t1, t2, t3, t4)
    count = rows.shape[0]
    base[...] = jnp.zeros(base.shape, jnp.float32)
    peak[...] = jnp.full(peak.shape, NEG, jnp.float32)
    for p in range(WINDOW):
        sq = jnp.square(targets[p][...].astype(jnp.float32))
        sq = sum(sq[:, q * LANES : (q + 1) * LANES] for q in range(sq.shape[1] // LANES))
        bias = jnp.concatenate(
            [
                jnp.sum(sq[r * LANES : (r + 1) * LANES, :].T, axis=0, keepdims=True)
                for r in range(count // LANES)
            ],
            axis=1,
        )
        bias = -KAPPA * bias
        bias = jnp.where(is_listed(mask, p), bias, NEG)
        base[p : p + 1, :] = bias

        block = dot_nt(rows[...], targets[p][...]) * TWO_KAPPA + bias
        entries[:, p * count : (p + 1) * count] = block
        best = peak[...]
        for q in range(count // LANES):
            best = jnp.maximum(best, block[:, q * LANES : (q + 1) * LANES])
        peak[...] = best

    col[...] = jnp.zeros(col.shape, jnp.float32)
    width = WINDOW * count // LANES

    def rows_of(r):
        return pl.ds(pl.multiple_of(r * LANES, LANES), LANES)

    def exponentials(r, meanwhile):
        here = rows_of(r)
        top = jnp.broadcast_to(jnp.max(peak[here, :], axis=1, keepdims=True), (LANES, LANES))
        acc = jnp.zeros((LANES, LANES), jnp.float32)
        for q in range(width):
            e = jnp.exp2(entries[here, q * LANES : (q + 1) * LANES] - top)
            entries[here, q * LANES : (q + 1) * LANES] = e
            acc = acc + e
        total = jnp.broadcast_to(jnp.sum(acc, axis=1, keepdims=True), (LANES, LANES))
        meanwhile()
        top_out[here, :] = top
        dual[here, :] = -(top + jnp.log2(total))
        peak[here, :] = 1.0 / total

    def columns(r):
        add_columns(entries, rows_of(r), peak[rows_of(r), :], col, width)

    def both(r, carry):
        exponentials(r, lambda: columns(r - 1))
        return carry

    exponentials(0, lambda: None)
    lax.fori_loop(1, count // LANES, both, 0)
    columns(count // LANES - 1)
    fine = put_columns(mask, base, col, sums_out, jnp.ones((1, LANES), jnp.float32))

    @pl.when(jnp.logical_not(fine))
    def _():
        put_exact_columns(mask, lambda p: (rows, targets[p]), dual, sums_out)


def later_kernel(
    mask, entries, pot, base, top, rows_far, t0, t1, t2, t3, t4, sums_out, dual_out, gain, col, low, total, rows, target
):
    targets = (t0, t1, t2, t3, t4)
    count = rows.shape[0]

    def fetch(p):
        pltpu.sync_copy(rows_far, rows)
        pltpu.sync_copy(targets[p], target)
        return rows, target

    col[...] = jnp.zeros(col.shape, jnp.float32)
    width = WINDOW * count // LANES
    worst = jnp.zeros((1, count), jnp.float32)
    for p in range(WINDOW):
        taken = is_listed(mask, p)
        shift = jnp.where(taken, pot[p : p + 1, :] - base[p : p + 1, :], 0.0)
        worst = jnp.maximum(worst, jnp.abs(shift))
        gain[:, p * count : (p + 1) * count] = jnp.broadcast_to(
            jnp.where(taken, jnp.exp2(shift), 0.0), (8, count)
        )
    low[...] = jnp.full(low.shape, 1.0, jnp.float32)

    def rows_of(r):
        return pl.ds(pl.multiple_of(r * LANES, LANES), LANES)

    def weigh(r, meanwhile):
        here = rows_of(r)
        acc = jnp.zeros((LANES, LANES), jnp.float32)
        for q in range(width):
            at = slice(q * LANES, (q + 1) * LANES)
            acc = acc + entries[here, at] * gain[0:1, at]
        mass = jnp.broadcast_to(jnp.sum(acc, axis=1, keepdims=True), (LANES, LANES))
        meanwhile()
        low[...] = jnp.minimum(low[...], mass)
        dual_out[here, :] = -(top[here, :] + jnp.log2(mass))
        total[here, :] = 1.0 / mass

    def columns(r):
        add_columns(entries, rows_of(r), total[rows_of(r), :], col, width)

    def both(r, carry):
        weigh(r, lambda: columns(r - 1))
        return carry

    weigh(0, lambda: None)
    lax.fori_loop(1, count // LANES, both, 0)
    columns(count // LANES - 1)
    fine = jnp.where(jnp.min(low[...], axis=0, keepdims=True) >= SAFE_ROW, 1.0, 0.0)
    for q in range(count // LANES):
        fine = jnp.minimum(fine, jnp.where(worst[:, q * LANES : (q + 1) * LANES] <= SAFE_SHIFT, 1.0, 0.0))
    fine = put_columns(mask, base, col, sums_out, fine)

    @pl.when(jnp.logical_not(fine))
    def _():
        def value(p, here):
            bias = jnp.where(is_listed(mask, p), pot[p : p + 1, :], NEG)
            return dot_nt(rows[here, :], target[...]) * TWO_KAPPA + bias

        dual_out[...] = jnp.full(dual_out.shape, NEG, jnp.float32)
        for p in range(WINDOW):
            fetch(p)

            def find(r, carry, p=p):
                here = pl.ds(pl.multiple_of(r * LANES, LANES), LANES)
                best = jnp.max(value(p, here), axis=1, keepdims=True)
                dual_out[here, :] = jnp.maximum(dual_out[here, :], best)
                return carry

            lax.fori_loop(0, count // LANES, find, 0)
        total[...] = jnp.zeros(total.shape, jnp.float32)
        for p in range(WINDOW):
            fetch(p)

            def add(r, carry, p=p):
                here = pl.ds(pl.multiple_of(r * LANES, LANES), LANES)
                e = jnp.exp2(value(p, here) - dual_out[here, 0:1])
                total[here, :] += jnp.sum(e, axis=1, keepdims=True)
                return carry

            lax.fori_loop(0, count // LANES, add, 0)
        dual_out[...] = -(dual_out[...] + jnp.log2(total[...]))

        put_exact_columns(mask, fetch, dual_out, sums_out)

    for r in range(count // LANES):
        here = slice(r * LANES, (r + 1) * LANES)
        sums_out[6:7, here] = dual_out[here, :].T[0:1, :]
    lane = lax.broadcasted_iota(jnp.int32, (1, LANES), 1)
    pairs = jnp.zeros((1, LANES), jnp.float32)
    for k in range(WINDOW):
        pairs = jnp.where(lane == k, mask[0, k].astype(jnp.float32), pairs)
    sums_out[7:8, 0:LANES] = pairs


VMEM = pl.BlockSpec(memory_space=pltpu.VMEM)
ANY = pl.BlockSpec(memory_space=pl.ANY)
SMEM = pl.BlockSpec(memory_space=pltpu.SMEM)


def first_step(mask, rows, targets):
    count, width = rows.shape
    pairs = WINDOW * count * count
    row = jax.ShapeDtypeStruct((8, count), jnp.float32)
    column = jax.ShapeDtypeStruct((count, LANES), jnp.float32)
    return pl.pallas_call(
        first_kernel,
        out_shape=(pltpu.VMEM((count, WINDOW * count), jnp.float32), row, column, row),
        in_specs=[SMEM] + [VMEM] * 6,
        out_specs=(VMEM,) * 4,
        scratch_shapes=[
            pltpu.VMEM((count, LANES), jnp.float32),
            pltpu.VMEM((count, LANES), jnp.float32),
            pltpu.VMEM((8, WINDOW * count), jnp.float32),
        ],
        compiler_params=pltpu.CompilerParams(vmem_limit_bytes=SCOPED),
        cost_estimate=pl.CostEstimate(
            flops=2 * pairs * width, bytes_accessed=12 * count * width, transcendentals=pairs
        ),
        name="first_step",
    )(mask, rows, *targets)


def later_step(mask, entries, pot, base, top, rows, targets):
    count, width = rows.shape
    pairs = WINDOW * count * count
    row = jax.ShapeDtypeStruct((8, count), jnp.float32)
    column = jax.ShapeDtypeStruct((count, LANES), jnp.float32)
    entries = pltpu.with_memory_space_constraint(entries, pltpu.VMEM)
    return pl.pallas_call(
        later_kernel,
        out_shape=(row, column),
        in_specs=[SMEM] + [VMEM] * 4 + [ANY] * 6,
        out_specs=(VMEM, VMEM),
        scratch_shapes=[
            pltpu.VMEM((8, WINDOW * count), jnp.float32),
            pltpu.VMEM((8, WINDOW * count), jnp.float32),
            pltpu.VMEM((LANES, LANES), jnp.float32),
            pltpu.VMEM((count, LANES), jnp.float32),
            pltpu.VMEM((count, width), jnp.bfloat16),
            pltpu.VMEM((count, width), jnp.bfloat16),
        ],
        compiler_params=pltpu.CompilerParams(vmem_limit_bytes=SCOPED),
        cost_estimate=pl.CostEstimate(
            flops=4 * pairs, bytes_accessed=12 * count * width, transcendentals=0
        ),
        name="later_step",
    )(mask, entries, pot, base, top, rows, *targets)


def grad_kernel(
    mask, pot, dual, around, mine, own, t0, t1, t2, t3, t4, x0, x1, x2, x3, x4, source_out, target_out
):
    targets = (t0, t1, t2, t3, t4)
    sources = (x0, x1, x2, x3, x4)
    width = own.shape[1]
    here = pl.ds(pl.multiple_of(lax.axis_index("grp") * LANES, LANES), LANES)
    dual_column = dual[here, 0:1]
    mass = jnp.zeros((LANES, 1), jnp.float32)
    carried = jnp.zeros((LANES, width), jnp.float32)
    for p in range(WINDOW):
        bias = jnp.where(is_listed(mask, p), pot[p : p + 1, :], NEG)
        weight = jnp.exp2(dot_nt(mine[...], targets[p][...]) * TWO_KAPPA + (dual_column + bias))
        weight = weight.astype(jnp.bfloat16)
        mass = mass + jnp.sum(weight.astype(jnp.float32), axis=1, keepdims=True)
        carried = carried + jnp.dot(weight, targets[p][...], preferred_element_type=jnp.float32)
    source_out[...] = 2.0 * (mine[...].astype(jnp.float32) * mass - carried)

    bias = jnp.broadcast_to(pot[0:1, here], (LANES, LANES)).T[:, 0:1]
    lane = lax.broadcasted_iota(jnp.int32, (1, LANES), 1)
    mass = jnp.zeros((LANES, 1), jnp.float32)
    pulled = jnp.zeros((LANES, width), jnp.float32)
    for p in range(WINDOW):
        low, high = ((2, 2), (1, 3), (3, 1), (0, 0), (4, 4))[p]
        slot = jnp.where(is_even(), low, high)
        taken = jnp.max(jnp.where(lane == slot, around[p, 1:2, 0:LANES], 0.0), axis=1, keepdims=True)
        shift = jnp.where(taken > 0.5, around[p, 0:1, :], NEG) + bias
        weight = jnp.exp2(dot_nt(own[...], sources[p][...]) * TWO_KAPPA + shift)
        weight = weight.astype(jnp.bfloat16)
        mass = mass + jnp.sum(weight.astype(jnp.float32), axis=1, keepdims=True)
        pulled = pulled + jnp.dot(weight, sources[p][...], preferred_element_type=jnp.float32)
    target_out[...] = 2.0 * (own[...].astype(jnp.float32) * mass - pulled)


def gradients(mask, pot, dual, around, mine, own, targets, sources):
    width = mine.shape[1]
    count = sources[0].shape[0]
    part = jax.ShapeDtypeStruct((LANES, width), jnp.float32)
    pairs = 2 * WINDOW * count * LANES
    return pl.pallas_call(
        grad_kernel,
        out_shape=(part, part),
        in_specs=[SMEM] + [VMEM] * 15,
        out_specs=(VMEM, VMEM),
        compiler_params=pltpu.CompilerParams(vmem_limit_bytes=SCOPED),
        cost_estimate=pl.CostEstimate(
            flops=4 * pairs * width, bytes_accessed=20 * count * width, transcendentals=pairs
        ),
        name="plan_gradients",
    )(mask, pot, dual, around, mine, own, *targets, *sources)


def neighbours(block, even):
    above = shifted(block, -2)
    below = shifted(block, 2)
    mate = swap_mate(block)
    cross = swap_mate(jnp.where(even, above, below))
    return block, mate, cross, above, below


def shards(source, target, pair_mask):
    row = lax.axis_index("row")
    even = row % 2 == 0
    targets = neighbours(gathered(target), even)
    rows = gathered(source)
    entries, partial, top, base = first_step(pair_mask, rows, targets)
    above = shifted(rows, -2)
    below = shifted(rows, 2)
    mate = swap_mate(rows)
    partial, above, below, mate = lax.optimization_barrier((partial, above, below, mate))
    cross = swap_mate(jnp.where(even, above, below))
    pot = -column_totals(partial, row)
    pot, cross = lax.optimization_barrier((pot, cross))
    sources = (rows, mate, cross, above, below)
    for _ in range(ITERS - 2):
        partial, dual = later_step(pair_mask, entries, pot, base, top, rows, targets)
        pot = -column_totals(partial, row)
    partial, dual = later_step(pair_mask, entries, pot, base, top, rows, targets)
    total, around = column_totals(partial, row, True)
    return gradients(pair_mask, -total, dual, around, source, target, targets, sources)


def solution(mesh):
    placed = (P(("row", "grp"), None), P(("row", "grp"), None), P("row", None))
    return jax.shard_map(
        shards,
        mesh=mesh,
        in_specs=placed,
        out_specs=(P(("row", "grp"), None), P(("row", "grp"), None)),
        check_vma=False,
    )
```

```python
import functools
import math

import jax
import jax.numpy as jnp
from jax import lax
from jax.experimental import pallas as pl
from jax.experimental.pallas import tpu as pltpu
from jax.sharding import PartitionSpec as P

EPS = 0.1
NEG = -1e30
KAPPA = 1.0 / (EPS * math.log(2.0))
TWO_KAPPA = 2.0 * KAPPA
SAFE_SUM = 2.0 ** -60
SAFE_ROW = 2.0 ** -28
SAFE_SHIFT = 60.0
SCOPED = 16 * 1024 * 1024
LANES = 128
WINDOW = 5


def from_row(block, source_of):
    count = lax.axis_size("row")
    return lax.ppermute(block, "row", [(source_of(i), i) for i in range(count)])


def swap_mate(block):
    return from_row(block, lambda i: i ^ 1)


def shifted(block, distance):
    count = lax.axis_size("row")
    return from_row(block, lambda i: (i - distance) % count)


def swap_chips(block, second):
    count = lax.axis_size("row")

    def source_of(i):
        chip, core = divmod(i, 2)
        reach = 1 + core
        up = (chip // reach) % 2 == 0
        if second:
            up = not up
        return (i + 2 * reach if up else i - 2 * reach) % count

    return from_row(block, source_of)


def gathered(shard):
    count = lax.axis_size("grp")
    copies = jnp.broadcast_to(shard[None], (count,) + shard.shape)
    return lax.all_to_all(copies, "grp", 0, 0, tiled=True).reshape(-1, shard.shape[1])


def lse2(a, b):
    top = jnp.maximum(a, b)
    return top + jnp.log2(jnp.exp2(a - top) + jnp.exp2(b - top))


def column_totals(partial, even, up, extra=False, cargo=None, movers=(), late=False):
    count = 2 if extra else 0
    other = swap_mate(partial[: 6 + count])
    chip = lse2(partial[:6], other[:6])
    if movers:
        chip, cargo = lax.optimization_barrier((chip, cargo))
    to_above, to_below = chip[2:6], chip[0:4]
    if count:
        mine = partial[6:8]
        here = jnp.where(
            even, jnp.concatenate([mine, other[6:]]), jnp.concatenate([other[6:], mine])
        )
        to_above = jnp.concatenate([to_above, here])
        to_below = jnp.concatenate([to_below, here])
    one = swap_chips(jnp.where(up, to_above, to_below), False)
    two = swap_chips(jnp.where(up, to_below, to_above), True)
    above = jnp.where(up, one, two)
    below = jnp.where(up, two, one)
    blank = jnp.full_like(above[0:2], NEG)
    outer = jnp.where(
        even,
        jnp.concatenate([below[0:2], lse2(below[2:4], above[0:2]), above[2:4]]),
        jnp.concatenate([below[2:4], blank, above[0:2]]),
    )
    sent = jnp.concatenate([outer, below[4:], above[4:]]) if count else outer
    got = swap_mate(sent)
    total = lse2(chip, lse2(outer, got[:6]))
    if movers:
        moved = [move(*cargo) for move in movers]
        if not late:
            total, moved = lax.optimization_barrier((total, moved))

    def placed(rows):
        return jnp.where(
            even,
            jnp.stack([rows[2], rows[3], rows[1], rows[4], rows[0]]),
            jnp.stack([rows[3], rows[2], rows[4], rows[5], rows[1]]),
        )

    if movers:
        return placed(total), moved
    if not count:
        return placed(total)
    near = jnp.where(even, sent[6:], got[6:])
    around = jnp.concatenate([near[:4], here, near[4:]]).reshape(6, count, -1)
    return placed(total), placed(around)


def dot_nt(a, b):
    return lax.dot_general(a, b, (((1,), (1,)), ((), ())), preferred_element_type=jnp.float32)


def exact_columns(rows, target, dual):
    count = rows.shape[0]

    def value(r):
        here = pl.ds(pl.multiple_of(r * LANES, LANES), LANES)
        return dot_nt(rows[here, :], target[...]) * TWO_KAPPA + dual[here, 0:1]

    def find(r, best):
        return jnp.maximum(best, jnp.max(value(r), axis=0, keepdims=True))

    best = lax.fori_loop(0, count // LANES, find, jnp.full((1, count), NEG, jnp.float32))

    def add(r, acc):
        return acc + jnp.sum(jnp.exp2(value(r) - best), axis=0, keepdims=True)

    acc = lax.fori_loop(0, count // LANES, add, jnp.zeros((1, count), jnp.float32))
    return best + jnp.log2(acc)


def is_even():
    return lax.rem(lax.axis_index("row"), 2) == 0


def place(p):
    low, high = ((2, 3), (3, 2), (1, 4), (4, 5), (0, 1))[p]
    return pl.ds(jnp.where(is_even(), low, high), 1)


def is_listed(mask, p):
    low, high = ((2, 2), (3, 1), (1, 3), (4, 4), (0, 0))[p]
    return mask[0, jnp.where(is_even(), low, high)] == 1


def put_columns(mask, base, col, sums_out, fine):
    count = sums_out.shape[1]
    sums_out[...] = jnp.full(sums_out.shape, NEG, jnp.float32)
    for p in range(WINDOW):
        sums = jnp.sum(col[:, p * count : (p + 1) * count], axis=0, keepdims=True)
        taken = is_listed(mask, p)
        sums_out[place(p), :] = jnp.where(taken, jnp.log2(sums) - base[p : p + 1, :], NEG)
        good = jnp.where(jnp.logical_or(jnp.logical_not(taken), sums >= SAFE_SUM), 1.0, 0.0)
        for q in range(count // LANES):
            fine = jnp.minimum(fine, good[:, q * LANES : (q + 1) * LANES])
    return jnp.min(fine) > 0.5


def put_exact_columns(mask, fetch, dual, sums_out):
    for p in range(WINDOW):

        @pl.when(is_listed(mask, p))
        def _(p=p):
            sums_out[place(p), :] = exact_columns(*fetch(p), dual)


def add_columns(entries, here, scale, col, width):
    for q in range(width):
        e = entries[here, q * LANES : (q + 1) * LANES] * scale
        col[:, q * LANES : (q + 1) * LANES] += jnp.sum(e.reshape(LANES // 8, 8, LANES), axis=0)


def first_kernel(mask, rows, t0, t1, t2, t3, t4, entries, sums_out, top_out, base, dual, peak, col):
    targets = (t0, t1, t2, t3, t4)
    count = rows.shape[0]
    base[...] = jnp.zeros(base.shape, jnp.float32)
    peak[...] = jnp.full(peak.shape, NEG, jnp.float32)
    for p in range(WINDOW):
        sq = jnp.square(targets[p][...].astype(jnp.float32))
        sq = sum(sq[:, q * LANES : (q + 1) * LANES] for q in range(sq.shape[1] // LANES))
        bias = jnp.concatenate(
            [
                jnp.sum(sq[r * LANES : (r + 1) * LANES, :].T, axis=0, keepdims=True)
                for r in range(count // LANES)
            ],
            axis=1,
        )
        bias = -KAPPA * bias
        bias = jnp.where(is_listed(mask, p), bias, NEG)
        base[p : p + 1, :] = bias

        block = dot_nt(rows[...], targets[p][...]) * TWO_KAPPA + bias
        entries[:, p * count : (p + 1) * count] = block
        best = peak[...]
        for q in range(count // LANES):
            best = jnp.maximum(best, block[:, q * LANES : (q + 1) * LANES])
        peak[...] = best

    col[...] = jnp.zeros(col.shape, jnp.float32)
    width = WINDOW * count // LANES

    def rows_of(r):
        return pl.ds(pl.multiple_of(r * LANES, LANES), LANES)

    def exponentials(r, meanwhile):
        here = rows_of(r)
        top = jnp.broadcast_to(jnp.max(peak[here, :], axis=1, keepdims=True), (LANES, LANES))
        acc = jnp.zeros((LANES, LANES), jnp.float32)
        for q in range(width):
            e = jnp.exp2(entries[here, q * LANES : (q + 1) * LANES] - top)
            entries[here, q * LANES : (q + 1) * LANES] = e
            acc = acc + e
        total = jnp.broadcast_to(jnp.sum(acc, axis=1, keepdims=True), (LANES, LANES))
        meanwhile()
        top_out[here, :] = top
        dual[here, :] = -(top + jnp.log2(total))
        peak[here, :] = 1.0 / total

    def columns(r):
        add_columns(entries, rows_of(r), peak[rows_of(r), :], col, width)

    def both(r, carry):
        exponentials(r, lambda: columns(r - 1))
        return carry

    exponentials(0, lambda: None)
    lax.fori_loop(1, count // LANES, both, 0)
    columns(count // LANES - 1)
    fine = put_columns(mask, base, col, sums_out, jnp.ones((1, LANES), jnp.float32))

    @pl.when(jnp.logical_not(fine))
    def _():
        put_exact_columns(mask, lambda p: (rows, targets[p]), dual, sums_out)


def later_kernel(
    mask, entries, pot, base, top, rows_far, t0, t1, t2, t3, t4, sums_out, dual_out, gain, col, low, total, rows, target
):
    targets = (t0, t1, t2, t3, t4)
    count = rows.shape[0]

    def fetch(p):
        pltpu.sync_copy(rows_far, rows)
        pltpu.sync_copy(targets[p], target)
        return rows, target

    col[...] = jnp.zeros(col.shape, jnp.float32)
    width = WINDOW * count // LANES
    worst = jnp.zeros((1, count), jnp.float32)
    for p in range(WINDOW):
        taken = is_listed(mask, p)
        shift = jnp.where(taken, pot[p : p + 1, :] - base[p : p + 1, :], 0.0)
        worst = jnp.maximum(worst, jnp.abs(shift))
        gain[:, p * count : (p + 1) * count] = jnp.broadcast_to(
            jnp.where(taken, jnp.exp2(shift), 0.0), (8, count)
        )
    low[...] = jnp.full(low.shape, 1.0, jnp.float32)

    def rows_of(r):
        return pl.ds(pl.multiple_of(r * LANES, LANES), LANES)

    def weigh(r, meanwhile):
        here = rows_of(r)
        acc = jnp.zeros((LANES, LANES), jnp.float32)
        for q in range(width):
            at = slice(q * LANES, (q + 1) * LANES)
            acc = acc + entries[here, at] * gain[0:1, at]
        mass = jnp.broadcast_to(jnp.sum(acc, axis=1, keepdims=True), (LANES, LANES))
        meanwhile()
        low[...] = jnp.minimum(low[...], mass)
        dual_out[here, :] = -(top[here, :] + jnp.log2(mass))
        total[here, :] = 1.0 / mass

    def columns(r):
        add_columns(entries, rows_of(r), total[rows_of(r), :], col, width)

    def both(r, carry):
        weigh(r, lambda: columns(r - 1))
        return carry

    weigh(0, lambda: None)
    lax.fori_loop(1, count // LANES, both, 0)
    columns(count // LANES - 1)
    fine = jnp.where(jnp.min(low[...], axis=0, keepdims=True) >= SAFE_ROW, 1.0, 0.0)
    for q in range(count // LANES):
        fine = jnp.minimum(fine, jnp.where(worst[:, q * LANES : (q + 1) * LANES] <= SAFE_SHIFT, 1.0, 0.0))
    fine = put_columns(mask, base, col, sums_out, fine)

    @pl.when(jnp.logical_not(fine))
    def _():
        def value(p, here):
            bias = jnp.where(is_listed(mask, p), pot[p : p + 1, :], NEG)
            return dot_nt(rows[here, :], target[...]) * TWO_KAPPA + bias

        dual_out[...] = jnp.full(dual_out.shape, NEG, jnp.float32)
        for p in range(WINDOW):
            fetch(p)

            def find(r, carry, p=p):
                here = pl.ds(pl.multiple_of(r * LANES, LANES), LANES)
                best = jnp.max(value(p, here), axis=1, keepdims=True)
                dual_out[here, :] = jnp.maximum(dual_out[here, :], best)
                return carry

            lax.fori_loop(0, count // LANES, find, 0)
        total[...] = jnp.zeros(total.shape, jnp.float32)
        for p in range(WINDOW):
            fetch(p)

            def add(r, carry, p=p):
                here = pl.ds(pl.multiple_of(r * LANES, LANES), LANES)
                e = jnp.exp2(value(p, here) - dual_out[here, 0:1])
                total[here, :] += jnp.sum(e, axis=1, keepdims=True)
                return carry

            lax.fori_loop(0, count // LANES, add, 0)
        dual_out[...] = -(dual_out[...] + jnp.log2(total[...]))

        put_exact_columns(mask, fetch, dual_out, sums_out)

    for r in range(count // LANES):
        here = slice(r * LANES, (r + 1) * LANES)
        sums_out[6:7, here] = dual_out[here, :].T[0:1, :]
    lane = lax.broadcasted_iota(jnp.int32, (1, LANES), 1)
    pairs = jnp.zeros((1, LANES), jnp.float32)
    for k in range(WINDOW):
        pairs = jnp.where(lane == k, mask[0, k].astype(jnp.float32), pairs)
    sums_out[7:8, 0:LANES] = pairs


VMEM = pl.BlockSpec(memory_space=pltpu.VMEM)
ANY = pl.BlockSpec(memory_space=pl.ANY)
SMEM = pl.BlockSpec(memory_space=pltpu.SMEM)


def first_step(mask, rows, targets):
    count, width = rows.shape
    pairs = WINDOW * count * count
    row = jax.ShapeDtypeStruct((8, count), jnp.float32)
    column = jax.ShapeDtypeStruct((count, LANES), jnp.float32)
    return pl.pallas_call(
        first_kernel,
        out_shape=(pltpu.VMEM((count, WINDOW * count), jnp.float32), row, column, row),
        in_specs=[SMEM] + [VMEM] * 6,
        out_specs=(VMEM,) * 4,
        scratch_shapes=[
            pltpu.VMEM((count, LANES), jnp.float32),
            pltpu.VMEM((count, LANES), jnp.float32),
            pltpu.VMEM((8, WINDOW * count), jnp.float32),
        ],
        compiler_params=pltpu.CompilerParams(vmem_limit_bytes=SCOPED),
        cost_estimate=pl.CostEstimate(
            flops=2 * pairs * width, bytes_accessed=12 * count * width, transcendentals=pairs
        ),
        name="first_step",
    )(mask, rows, *targets)


def later_step(mask, entries, pot, base, top, rows, targets):
    count, width = rows.shape
    pairs = WINDOW * count * count
    row = jax.ShapeDtypeStruct((8, count), jnp.float32)
    column = jax.ShapeDtypeStruct((count, LANES), jnp.float32)
    entries = pltpu.with_memory_space_constraint(entries, pltpu.VMEM)
    return pl.pallas_call(
        later_kernel,
        out_shape=(row, column),
        in_specs=[SMEM] + [VMEM] * 4 + [ANY] * 6,
        out_specs=(VMEM, VMEM),
        scratch_shapes=[
            pltpu.VMEM((8, WINDOW * count), jnp.float32),
            pltpu.VMEM((8, WINDOW * count), jnp.float32),
            pltpu.VMEM((LANES, LANES), jnp.float32),
            pltpu.VMEM((count, LANES), jnp.float32),
            pltpu.VMEM((count, width), jnp.bfloat16),
            pltpu.VMEM((count, width), jnp.bfloat16),
        ],
        compiler_params=pltpu.CompilerParams(vmem_limit_bytes=SCOPED),
        cost_estimate=pl.CostEstimate(
            flops=4 * pairs, bytes_accessed=12 * count * width, transcendentals=0
        ),
        name="later_step",
    )(mask, entries, pot, base, top, rows, *targets)


def grad_kernel(
    mask, pot, dual, around, mine, own, t0, t1, t2, t3, t4, x0, x1, x2, x3, x4, source_out, target_out
):
    targets = (t0, t1, t2, t3, t4)
    sources = (x0, x1, x2, x3, x4)
    width = own.shape[1]
    here = pl.ds(pl.multiple_of(lax.axis_index("grp") * LANES, LANES), LANES)
    dual_column = dual[here, 0:1]
    mass = jnp.zeros((LANES, 1), jnp.float32)
    carried = jnp.zeros((LANES, width), jnp.float32)
    for p in range(WINDOW):
        bias = jnp.where(is_listed(mask, p), pot[p : p + 1, :], NEG)
        weight = jnp.exp2(dot_nt(mine[...], targets[p][...]) * TWO_KAPPA + (dual_column + bias))
        weight = weight.astype(jnp.bfloat16)
        mass = mass + jnp.sum(weight.astype(jnp.float32), axis=1, keepdims=True)
        carried = carried + jnp.dot(weight, targets[p][...], preferred_element_type=jnp.float32)
    source_out[...] = 2.0 * (mine[...].astype(jnp.float32) * mass - carried)

    bias = jnp.broadcast_to(pot[0:1, here], (LANES, LANES)).T[:, 0:1]
    lane = lax.broadcasted_iota(jnp.int32, (1, LANES), 1)
    mass = jnp.zeros((LANES, 1), jnp.float32)
    pulled = jnp.zeros((LANES, width), jnp.float32)
    for p in range(WINDOW):
        low, high = ((2, 2), (1, 3), (3, 1), (0, 0), (4, 4))[p]
        slot = jnp.where(is_even(), low, high)
        taken = jnp.max(jnp.where(lane == slot, around[p, 1:2, 0:LANES], 0.0), axis=1, keepdims=True)
        shift = jnp.where(taken > 0.5, around[p, 0:1, :], NEG) + bias
        weight = jnp.exp2(dot_nt(own[...], sources[p][...]) * TWO_KAPPA + shift)
        weight = weight.astype(jnp.bfloat16)
        mass = mass + jnp.sum(weight.astype(jnp.float32), axis=1, keepdims=True)
        pulled = pulled + jnp.dot(weight, sources[p][...], preferred_element_type=jnp.float32)
    target_out[...] = 2.0 * (own[...].astype(jnp.float32) * mass - pulled)


def gradients(mask, pot, dual, around, mine, own, targets, sources):
    width = mine.shape[1]
    count = sources[0].shape[0]
    part = jax.ShapeDtypeStruct((LANES, width), jnp.float32)
    pairs = 2 * WINDOW * count * LANES
    return pl.pallas_call(
        grad_kernel,
        out_shape=(part, part),
        in_specs=[SMEM] + [VMEM] * 15,
        out_specs=(VMEM, VMEM),
        compiler_params=pltpu.CompilerParams(vmem_limit_bytes=SCOPED),
        cost_estimate=pl.CostEstimate(
            flops=4 * pairs * width, bytes_accessed=20 * count * width, transcendentals=pairs
        ),
        name="plan_gradients",
    )(mask, pot, dual, around, mine, own, *targets, *sources)


def neighbours(block, even):
    above = shifted(block, -2)
    below = shifted(block, 2)
    mate = swap_mate(block)
    cross = swap_mate(jnp.where(even, above, below))
    return block, mate, cross, above, below


def shards(source, target, pair_mask):
    row = lax.axis_index("row")
    even = row % 2 == 0
    up = (row // 2) // (1 + row % 2) % 2 == 0
    targets = neighbours(gathered(target), even)
    rows = gathered(source)
    rows, even, up = lax.optimization_barrier((rows, even, up))
    entries, partial, top, base = first_step(pair_mask, rows, targets)
    total, (above, below) = column_totals(
        partial, even, up, False, (rows,), (lambda x: shifted(x, -2), lambda x: shifted(x, 2)), True
    )
    partial, dual = later_step(pair_mask, entries, -total, base, top, rows, targets)
    total, (mate, cross) = column_totals(
        partial,
        even,
        up,
        False,
        (rows, above, below),
        (lambda x, a, b: swap_mate(x), lambda x, a, b: swap_mate(jnp.where(even, a, b))),
    )
    partial, dual = later_step(pair_mask, entries, -total, base, top, rows, targets)
    total, around = column_totals(partial, even, up, True)
    sources = (rows, mate, cross, above, below)
    return gradients(pair_mask, -total, dual, around, source, target, targets, sources)


def solution(mesh):
    placed = (P(("row", "grp"), None), P(("row", "grp"), None), P("row", None))
    return jax.shard_map(
        shards,
        mesh=mesh,
        in_specs=placed,
        out_specs=(P(("row", "grp"), None), P(("row", "grp"), None)),
        check_vma=False,
    )
```

```python
import functools
import math

import jax
import jax.numpy as jnp
from jax import lax
from jax.experimental import pallas as pl
from jax.experimental.pallas import tpu as pltpu
from jax.sharding import PartitionSpec as P

EPS = 0.1
NEG = -1e30
KAPPA = 1.0 / (EPS * math.log(2.0))
TWO_KAPPA = 2.0 * KAPPA
SAFE_SUM = 2.0 ** -60
SAFE_ROW = 2.0 ** -28
HIGH_ROW = 2.0 ** 60
SAFE_SHIFT = 60.0
SCOPED = 16 * 1024 * 1024
LANES = 128
WINDOW = 5


def from_row(block, source_of):
    count = lax.axis_size("row")
    return lax.ppermute(block, "row", [(source_of(i), i) for i in range(count)])


def swap_mate(block):
    return from_row(block, lambda i: i ^ 1)


def shifted(block, distance):
    count = lax.axis_size("row")
    return from_row(block, lambda i: (i - distance) % count)


def swap_chips(block, second):
    count = lax.axis_size("row")

    def source_of(i):
        chip, core = divmod(i, 2)
        reach = 1 + core
        up = (chip // reach) % 2 == 0
        if second:
            up = not up
        return (i + 2 * reach if up else i - 2 * reach) % count

    return from_row(block, source_of)


def gathered(shard):
    count = lax.axis_size("grp")
    copies = jnp.broadcast_to(shard[None], (count,) + shard.shape)
    return lax.all_to_all(copies, "grp", 0, 0, tiled=True).reshape(-1, shard.shape[1])


def lse2(a, b):
    top = jnp.maximum(a, b)
    return top + jnp.log2(jnp.exp2(a - top) + jnp.exp2(b - top))


def column_totals(partial, even, up, extra=False, cargo=None, movers=()):
    count = 2 if extra else 0
    other = swap_mate(partial[: 6 + count])
    chip = lse2(partial[:6], other[:6])
    if movers:
        chip, cargo = lax.optimization_barrier((chip, cargo))
    to_above, to_below = chip[2:6], chip[0:4]
    if count:
        mine = partial[6:8]
        here = jnp.where(
            even, jnp.concatenate([mine, other[6:]]), jnp.concatenate([other[6:], mine])
        )
        to_above = jnp.concatenate([to_above, here])
        to_below = jnp.concatenate([to_below, here])
    one = swap_chips(jnp.where(up, to_above, to_below), False)
    two = swap_chips(jnp.where(up, to_below, to_above), True)
    above = jnp.where(up, one, two)
    below = jnp.where(up, two, one)
    blank = jnp.full_like(above[0:2], NEG)
    outer = jnp.where(
        even,
        jnp.concatenate([below[0:2], lse2(below[2:4], above[0:2]), above[2:4]]),
        jnp.concatenate([below[2:4], blank, above[0:2]]),
    )
    sent = jnp.concatenate([outer, below[4:], above[4:]]) if count else outer
    got = swap_mate(sent)
    total = lse2(chip, lse2(outer, got[:6]))
    if movers:
        moved = [move(*cargo) for move in movers]
        total, moved = lax.optimization_barrier((total, moved))

    def placed(rows):
        return jnp.where(
            even,
            jnp.stack([rows[2], rows[3], rows[1], rows[4], rows[0]]),
            jnp.stack([rows[3], rows[2], rows[4], rows[5], rows[1]]),
        )

    if movers:
        return placed(total), moved
    if not count:
        return placed(total)
    near = jnp.where(even, sent[6:], got[6:])
    around = jnp.concatenate([near[:4], here, near[4:]]).reshape(6, count, -1)
    return placed(total), placed(around)


def dot_nt(a, b):
    return lax.dot_general(a, b, (((1,), (1,)), ((), ())), preferred_element_type=jnp.float32)


def exact_columns(rows, target, dual):
    count = rows.shape[0]

    def value(r):
        here = pl.ds(pl.multiple_of(r * LANES, LANES), LANES)
        return dot_nt(rows[here, :], target[...]) * TWO_KAPPA + dual[here, 0:1]

    def find(r, best):
        return jnp.maximum(best, jnp.max(value(r), axis=0, keepdims=True))

    best = lax.fori_loop(0, count // LANES, find, jnp.full((1, count), NEG, jnp.float32))

    def add(r, acc):
        return acc + jnp.sum(jnp.exp2(value(r) - best), axis=0, keepdims=True)

    acc = lax.fori_loop(0, count // LANES, add, jnp.zeros((1, count), jnp.float32))
    return best + jnp.log2(acc)


def is_even():
    return lax.rem(lax.axis_index("row"), 2) == 0


def place(p):
    low, high = ((2, 3), (3, 2), (1, 4), (4, 5), (0, 1))[p]
    return pl.ds(jnp.where(is_even(), low, high), 1)


def is_listed(mask, p):
    low, high = ((2, 2), (3, 1), (1, 3), (4, 4), (0, 0))[p]
    return mask[0, jnp.where(is_even(), low, high)] == 1


def put_columns(mask, base, col, sums_out, fine):
    count = sums_out.shape[1]
    sums_out[...] = jnp.full(sums_out.shape, NEG, jnp.float32)
    for p in range(WINDOW):
        sums = jnp.sum(col[:, p * count : (p + 1) * count], axis=0, keepdims=True)
        taken = is_listed(mask, p)
        sums_out[place(p), :] = jnp.where(taken, jnp.log2(sums) - base[p : p + 1, :], NEG)
        good = jnp.where(jnp.logical_or(jnp.logical_not(taken), sums >= SAFE_SUM), 1.0, 0.0)
        for q in range(count // LANES):
            fine = jnp.minimum(fine, good[:, q * LANES : (q + 1) * LANES])
    return jnp.min(fine) > 0.5


def put_exact_columns(mask, fetch, dual, sums_out):
    for p in range(WINDOW):

        @pl.when(is_listed(mask, p))
        def _(p=p):
            sums_out[place(p), :] = exact_columns(*fetch(p), dual)


def note_range(good, total):
    inside = jnp.logical_and(total >= SAFE_ROW, total <= HIGH_ROW)
    good[...] = jnp.minimum(good[...], jnp.where(inside, 1.0, 0.0))


def put_exact_rows(mask, fetch, bias, dual, total):
    count = dual.shape[0]

    def value(block, p, here):
        rows, target = block
        shift = jnp.where(is_listed(mask, p), bias[p : p + 1, :], NEG)
        return dot_nt(rows[here, :], target[...]) * TWO_KAPPA + shift

    dual[...] = jnp.full(dual.shape, NEG, jnp.float32)
    for p in range(WINDOW):
        block = fetch(p)

        def find(r, carry, p=p, block=block):
            here = pl.ds(pl.multiple_of(r * LANES, LANES), LANES)
            best = jnp.max(value(block, p, here), axis=1, keepdims=True)
            dual[here, :] = jnp.maximum(dual[here, :], best)
            return carry

        lax.fori_loop(0, count // LANES, find, 0)
    total[...] = jnp.zeros(total.shape, jnp.float32)
    for p in range(WINDOW):
        block = fetch(p)

        def add(r, carry, p=p, block=block):
            here = pl.ds(pl.multiple_of(r * LANES, LANES), LANES)
            e = jnp.exp2(value(block, p, here) - dual[here, 0:1])
            total[here, :] += jnp.sum(e, axis=1, keepdims=True)
            return carry

        lax.fori_loop(0, count // LANES, add, 0)
    dual[...] = -(dual[...] + jnp.log2(total[...]))


def add_columns(entries, here, scale, col, width):
    for q in range(width):
        e = entries[here, q * LANES : (q + 1) * LANES] * scale
        col[:, q * LANES : (q + 1) * LANES] += jnp.sum(e.reshape(LANES // 8, 8, LANES), axis=0)


def first_kernel(mask, rows, t0, t1, t2, t3, t4, entries, sums_out, top_out, base, dual, mass, good, col):
    targets = (t0, t1, t2, t3, t4)
    count = rows.shape[0]
    base[...] = jnp.zeros(base.shape, jnp.float32)
    for p in range(WINDOW):
        sq = jnp.square(targets[p][...].astype(jnp.float32))
        sq = sum(sq[:, q * LANES : (q + 1) * LANES] for q in range(sq.shape[1] // LANES))
        bias = jnp.concatenate(
            [
                jnp.sum(sq[r * LANES : (r + 1) * LANES, :].T, axis=0, keepdims=True)
                for r in range(count // LANES)
            ],
            axis=1,
        )
        bias = jnp.where(is_listed(mask, p), -KAPPA * bias, NEG)
        base[p : p + 1, :] = bias

    block = dot_nt(rows[...], targets[0][...]) * TWO_KAPPA + base[0:1, :]
    entries[:, 0:count] = block
    best = block[:, 0:LANES]
    for q in range(1, count // LANES):
        best = jnp.maximum(best, block[:, q * LANES : (q + 1) * LANES])
    top_out[...] = jnp.broadcast_to(jnp.max(best, axis=1, keepdims=True), (count, LANES))
    for p in (1, 2, 3, 4, 0):
        if p:
            block = dot_nt(rows[...], targets[p][...]) * TWO_KAPPA + base[p : p + 1, :]
        else:
            block = entries[:, 0:count]
        acc = jnp.zeros((count, LANES), jnp.float32) if p == 1 else mass[...]
        top = top_out[...]
        for q in range(count // LANES):
            e = jnp.exp2(block[:, q * LANES : (q + 1) * LANES] - top)
            entries[:, p * count + q * LANES : p * count + (q + 1) * LANES] = e
            acc = acc + e
        mass[...] = acc

    col[...] = jnp.zeros(col.shape, jnp.float32)
    good[...] = jnp.ones(good.shape, jnp.float32)
    width = WINDOW * count // LANES

    def rows_of(r):
        return pl.ds(pl.multiple_of(r * LANES, LANES), LANES)

    def invert(r, carry):
        here = rows_of(r)
        total = jnp.broadcast_to(jnp.sum(mass[here, :], axis=1, keepdims=True), (LANES, LANES))
        note_range(good, total)
        dual[here, :] = -(top_out[here, :] + jnp.log2(total))
        mass[here, :] = 1.0 / total
        return carry

    lax.fori_loop(0, count // LANES, invert, 0)

    def columns(r, carry):
        add_columns(entries, rows_of(r), mass[rows_of(r), :], col, width)
        return carry

    lax.fori_loop(0, count // LANES, columns, 0)
    fine = put_columns(mask, base, col, sums_out, jnp.min(good[...], axis=0, keepdims=True))

    @pl.when(jnp.logical_not(fine))
    def _():
        def fetch(p):
            return rows, targets[p]

        put_exact_rows(mask, fetch, base, dual, mass)
        put_exact_columns(mask, fetch, dual, sums_out)


def later_kernel(
    mask, entries, pot, base, top, rows_far, t0, t1, t2, t3, t4, sums_out, dual_out, gain, col, good, total, rows, target
):
    targets = (t0, t1, t2, t3, t4)
    count = rows.shape[0]

    def fetch(p):
        pltpu.sync_copy(rows_far, rows)
        pltpu.sync_copy(targets[p], target)
        return rows, target

    col[...] = jnp.zeros(col.shape, jnp.float32)
    width = WINDOW * count // LANES
    worst = jnp.zeros((1, count), jnp.float32)
    for p in range(WINDOW):
        taken = is_listed(mask, p)
        shift = jnp.where(taken, pot[p : p + 1, :] - base[p : p + 1, :], 0.0)
        worst = jnp.maximum(worst, jnp.abs(shift))
        gain[:, p * count : (p + 1) * count] = jnp.broadcast_to(
            jnp.where(taken, jnp.exp2(shift), 0.0), (8, count)
        )
    good[...] = jnp.ones(good.shape, jnp.float32)

    def rows_of(r):
        return pl.ds(pl.multiple_of(r * LANES, LANES), LANES)

    def weigh(r, meanwhile):
        here = rows_of(r)
        acc = jnp.zeros((LANES, LANES), jnp.float32)
        for q in range(width):
            at = slice(q * LANES, (q + 1) * LANES)
            acc = acc + entries[here, at] * gain[0:1, at]
        mass = jnp.broadcast_to(jnp.sum(acc, axis=1, keepdims=True), (LANES, LANES))
        meanwhile()
        note_range(good, mass)
        dual_out[here, :] = -(top[here, :] + jnp.log2(mass))
        total[here, :] = 1.0 / mass

    def columns(r):
        add_columns(entries, rows_of(r), total[rows_of(r), :], col, width)

    def both(r, carry):
        weigh(r, lambda: columns(r - 1))
        return carry

    weigh(0, lambda: None)
    lax.fori_loop(1, count // LANES, both, 0)
    columns(count // LANES - 1)
    fine = jnp.min(good[...], axis=0, keepdims=True)
    for q in range(count // LANES):
        fine = jnp.minimum(fine, jnp.where(worst[:, q * LANES : (q + 1) * LANES] <= SAFE_SHIFT, 1.0, 0.0))
    fine = put_columns(mask, base, col, sums_out, fine)

    @pl.when(jnp.logical_not(fine))
    def _():
        put_exact_rows(mask, fetch, pot, dual_out, total)
        put_exact_columns(mask, fetch, dual_out, sums_out)

    for r in range(count // LANES):
        here = slice(r * LANES, (r + 1) * LANES)
        sums_out[6:7, here] = dual_out[here, :].T[0:1, :]
    lane = lax.broadcasted_iota(jnp.int32, (1, LANES), 1)
    pairs = jnp.zeros((1, LANES), jnp.float32)
    for k in range(WINDOW):
        pairs = jnp.where(lane == k, mask[0, k].astype(jnp.float32), pairs)
    sums_out[7:8, 0:LANES] = pairs


VMEM = pl.BlockSpec(memory_space=pltpu.VMEM)
ANY = pl.BlockSpec(memory_space=pl.ANY)
SMEM = pl.BlockSpec(memory_space=pltpu.SMEM)


def first_step(mask, rows, targets):
    count, width = rows.shape
    pairs = WINDOW * count * count
    row = jax.ShapeDtypeStruct((8, count), jnp.float32)
    column = jax.ShapeDtypeStruct((count, LANES), jnp.float32)
    return pl.pallas_call(
        first_kernel,
        out_shape=(pltpu.VMEM((count, WINDOW * count), jnp.float32), row, column, row),
        in_specs=[SMEM] + [VMEM] * 6,
        out_specs=(VMEM,) * 4,
        scratch_shapes=[
            pltpu.VMEM((count, LANES), jnp.float32),
            pltpu.VMEM((count, LANES), jnp.float32),
            pltpu.VMEM((LANES, LANES), jnp.float32),
            pltpu.VMEM((8, WINDOW * count), jnp.float32),
        ],
        compiler_params=pltpu.CompilerParams(vmem_limit_bytes=SCOPED),
        cost_estimate=pl.CostEstimate(
            flops=2 * pairs * width, bytes_accessed=12 * count * width, transcendentals=pairs
        ),
        name="first_step",
    )(mask, rows, *targets)


def later_step(last, mask, entries, pot, base, top, rows, targets):
    count, width = rows.shape
    pairs = WINDOW * count * count
    row = jax.ShapeDtypeStruct((8, count), jnp.float32)
    column = jax.ShapeDtypeStruct((count, LANES), jnp.float32)
    entries = pltpu.with_memory_space_constraint(entries, pltpu.VMEM)
    out_shape = (row, column) if last else (row,)
    dual = [] if last else [pltpu.VMEM((count, LANES), jnp.float32)]
    return pl.pallas_call(
        later_kernel,
        out_shape=out_shape,
        in_specs=[SMEM] + [VMEM] * 4 + [ANY] * 6,
        out_specs=(VMEM,) * len(out_shape),
        scratch_shapes=dual
        + [
            pltpu.VMEM((8, WINDOW * count), jnp.float32),
            pltpu.VMEM((8, WINDOW * count), jnp.float32),
            pltpu.VMEM((LANES, LANES), jnp.float32),
            pltpu.VMEM((count, LANES), jnp.float32),
            pltpu.VMEM((count, width), jnp.bfloat16),
            pltpu.VMEM((count, width), jnp.bfloat16),
        ],
        compiler_params=pltpu.CompilerParams(vmem_limit_bytes=SCOPED),
        cost_estimate=pl.CostEstimate(
            flops=4 * pairs, bytes_accessed=12 * count * width, transcendentals=0
        ),
        name="later_step",
    )(mask, entries, pot, base, top, rows, *targets)


def grad_kernel(
    mask, pot, dual, around, mine, own, t0, t1, t2, t3, t4, x0, x1, x2, x3, x4, source_out, target_out
):
    targets = (t0, t1, t2, t3, t4)
    sources = (x0, x1, x2, x3, x4)
    width = own.shape[1]
    here = pl.ds(pl.multiple_of(lax.axis_index("grp") * LANES, LANES), LANES)
    dual_column = dual[here, 0:1]
    mass = jnp.zeros((LANES, 1), jnp.float32)
    carried = jnp.zeros((LANES, width), jnp.float32)
    for p in range(WINDOW):
        bias = jnp.where(is_listed(mask, p), pot[p : p + 1, :], NEG)
        weight = jnp.exp2(dot_nt(mine[...], targets[p][...]) * TWO_KAPPA + (dual_column + bias))
        weight = weight.astype(jnp.bfloat16)
        mass = mass + jnp.sum(weight.astype(jnp.float32), axis=1, keepdims=True)
        carried = carried + jnp.dot(weight, targets[p][...], preferred_element_type=jnp.float32)
    source_out[...] = 2.0 * (mine[...].astype(jnp.float32) * mass - carried)

    bias = jnp.broadcast_to(pot[0:1, here], (LANES, LANES)).T[:, 0:1]
    lane = lax.broadcasted_iota(jnp.int32, (1, LANES), 1)
    mass = jnp.zeros((LANES, 1), jnp.float32)
    pulled = jnp.zeros((LANES, width), jnp.float32)
    for p in range(WINDOW):
        low, high = ((2, 2), (1, 3), (3, 1), (0, 0), (4, 4))[p]
        slot = jnp.where(is_even(), low, high)
        taken = jnp.max(jnp.where(lane == slot, around[p, 1:2, 0:LANES], 0.0), axis=1, keepdims=True)
        shift = jnp.where(taken > 0.5, around[p, 0:1, :], NEG) + bias
        weight = jnp.exp2(dot_nt(own[...], sources[p][...]) * TWO_KAPPA + shift)
        weight = weight.astype(jnp.bfloat16)
        mass = mass + jnp.sum(weight.astype(jnp.float32), axis=1, keepdims=True)
        pulled = pulled + jnp.dot(weight, sources[p][...], preferred_element_type=jnp.float32)
    target_out[...] = 2.0 * (own[...].astype(jnp.float32) * mass - pulled)


def gradients(mask, pot, dual, around, mine, own, targets, sources):
    width = mine.shape[1]
    count = sources[0].shape[0]
    part = jax.ShapeDtypeStruct((LANES, width), jnp.float32)
    pairs = 2 * WINDOW * count * LANES
    return pl.pallas_call(
        grad_kernel,
        out_shape=(part, part),
        in_specs=[SMEM] + [VMEM] * 15,
        out_specs=(VMEM, VMEM),
        compiler_params=pltpu.CompilerParams(vmem_limit_bytes=SCOPED),
        cost_estimate=pl.CostEstimate(
            flops=4 * pairs * width, bytes_accessed=20 * count * width, transcendentals=pairs
        ),
        name="plan_gradients",
    )(mask, pot, dual, around, mine, own, *targets, *sources)


def neighbours(block, even):
    above = shifted(block, -2)
    below = shifted(block, 2)
    mate = swap_mate(block)
    cross = swap_mate(jnp.where(even, above, below))
    return block, mate, cross, above, below


def shards(source, target, pair_mask):
    row = lax.axis_index("row")
    even = row % 2 == 0
    up = (row // 2) // (1 + row % 2) % 2 == 0
    targets = neighbours(gathered(target), even)
    rows = gathered(source)
    rows, even, up = lax.optimization_barrier((rows, even, up))
    entries, partial, top, base = first_step(pair_mask, rows, targets)
    total, (above, below) = column_totals(
        partial, even, up, False, (rows,), (lambda x: shifted(x, -2), lambda x: shifted(x, 2))
    )
    (partial,) = later_step(False, pair_mask, entries, -total, base, top, rows, targets)
    total, (mate, cross) = column_totals(
        partial,
        even,
        up,
        False,
        (rows, above, below),
        (lambda x, a, b: swap_mate(x), lambda x, a, b: swap_mate(jnp.where(even, a, b))),
    )
    partial, dual = later_step(True, pair_mask, entries, -total, base, top, rows, targets)
    total, around = column_totals(partial, even, up, True)
    sources = (rows, mate, cross, above, below)
    return gradients(pair_mask, -total, dual, around, source, target, targets, sources)


def solution(mesh):
    placed = (P(("row", "grp"), None), P(("row", "grp"), None), P("row", None))
    return jax.shard_map(
        shards,
        mesh=mesh,
        in_specs=placed,
        out_specs=(P(("row", "grp"), None), P(("row", "grp"), None)),
        check_vma=False,
    )
```

```python
import functools
import math

import jax
import jax.numpy as jnp
from jax import lax
from jax.experimental import pallas as pl
from jax.experimental.pallas import tpu as pltpu
from jax.sharding import PartitionSpec as P

EPS = 0.1
NEG = -1e30
KAPPA = 1.0 / (EPS * math.log(2.0))
TWO_KAPPA = 2.0 * KAPPA
SAFE_SUM = 2.0 ** -60
SAFE_ROW = 2.0 ** -28
HIGH_ROW = 2.0 ** 60
SAFE_SHIFT = 60.0
SCOPED = 16 * 1024 * 1024
LANES = 128
WINDOW = 5


def from_row(block, source_of):
    count = lax.axis_size("row")
    return lax.ppermute(block, "row", [(source_of(i), i) for i in range(count)])


def swap_mate(block):
    return from_row(block, lambda i: i ^ 1)


def shifted(block, distance):
    count = lax.axis_size("row")
    return from_row(block, lambda i: (i - distance) % count)


def swap_chips(block, second):
    count = lax.axis_size("row")

    def source_of(i):
        chip, core = divmod(i, 2)
        reach = 1 + core
        up = (chip // reach) % 2 == 0
        if second:
            up = not up
        return (i + 2 * reach if up else i - 2 * reach) % count

    return from_row(block, source_of)


def gathered(shard):
    count = lax.axis_size("grp")
    copies = jnp.broadcast_to(shard[None], (count,) + shard.shape)
    return lax.all_to_all(copies, "grp", 0, 0, tiled=True).reshape(-1, shard.shape[1])


def lse2(a, b):
    top = jnp.maximum(a, b)
    return top + jnp.log2(jnp.exp2(a - top) + jnp.exp2(b - top))


def column_totals(partial, even, up, extra=False, cargo=None, movers=(), late=False):
    count = 2 if extra else 0
    other = swap_mate(partial[: 6 + count])
    chip = lse2(partial[:6], other[:6])
    if movers:
        chip, cargo = lax.optimization_barrier((chip, cargo))
    to_above, to_below = chip[2:6], chip[0:4]
    if count:
        mine = partial[6:8]
        here = jnp.where(
            even, jnp.concatenate([mine, other[6:]]), jnp.concatenate([other[6:], mine])
        )
        to_above = jnp.concatenate([to_above, here])
        to_below = jnp.concatenate([to_below, here])
    one = swap_chips(jnp.where(up, to_above, to_below), False)
    two = swap_chips(jnp.where(up, to_below, to_above), True)
    above = jnp.where(up, one, two)
    below = jnp.where(up, two, one)
    blank = jnp.full_like(above[0:2], NEG)
    outer = jnp.where(
        even,
        jnp.concatenate([below[0:2], lse2(below[2:4], above[0:2]), above[2:4]]),
        jnp.concatenate([below[2:4], blank, above[0:2]]),
    )
    sent = jnp.concatenate([outer, below[4:], above[4:]]) if count else outer
    got = swap_mate(sent)
    total = lse2(chip, lse2(outer, got[:6]))
    if movers:
        moved = [move(*cargo) for move in movers]
        if not late:
            total, moved = lax.optimization_barrier((total, moved))

    def placed(rows):
        return jnp.where(
            even,
            jnp.stack([rows[2], rows[3], rows[1], rows[4], rows[0]]),
            jnp.stack([rows[3], rows[2], rows[4], rows[5], rows[1]]),
        )

    if movers:
        return placed(total), moved
    if not count:
        return placed(total)
    near = jnp.where(even, sent[6:], got[6:])
    around = jnp.concatenate([near[:4], here, near[4:]]).reshape(6, count, -1)
    return placed(total), placed(around)


def dot_nt(a, b):
    return lax.dot_general(a, b, (((1,), (1,)), ((), ())), preferred_element_type=jnp.float32)


def exact_columns(rows, target, dual):
    count = rows.shape[0]

    def value(r):
        here = pl.ds(pl.multiple_of(r * LANES, LANES), LANES)
        return dot_nt(rows[here, :], target[...]) * TWO_KAPPA + dual[here, 0:1]

    def find(r, best):
        return jnp.maximum(best, jnp.max(value(r), axis=0, keepdims=True))

    best = lax.fori_loop(0, count // LANES, find, jnp.full((1, count), NEG, jnp.float32))

    def add(r, acc):
        return acc + jnp.sum(jnp.exp2(value(r) - best), axis=0, keepdims=True)

    acc = lax.fori_loop(0, count // LANES, add, jnp.zeros((1, count), jnp.float32))
    return best + jnp.log2(acc)


def is_even():
    return lax.rem(lax.axis_index("row"), 2) == 0


def place(p):
    low, high = ((2, 3), (3, 2), (1, 4), (4, 5), (0, 1))[p]
    return pl.ds(jnp.where(is_even(), low, high), 1)


def is_listed(mask, p):
    low, high = ((2, 2), (3, 1), (1, 3), (4, 4), (0, 0))[p]
    return mask[0, jnp.where(is_even(), low, high)] == 1


def put_columns(mask, base, col, sums_out, fine):
    count = sums_out.shape[1]
    sums_out[...] = jnp.full(sums_out.shape, NEG, jnp.float32)
    for p in range(WINDOW):
        sums = jnp.sum(col[:, p * count : (p + 1) * count], axis=0, keepdims=True)
        taken = is_listed(mask, p)
        sums_out[place(p), :] = jnp.where(taken, jnp.log2(sums) - base[p : p + 1, :], NEG)
        good = jnp.where(jnp.logical_or(jnp.logical_not(taken), sums >= SAFE_SUM), 1.0, 0.0)
        for q in range(count // LANES):
            fine = jnp.minimum(fine, good[:, q * LANES : (q + 1) * LANES])
    return jnp.min(fine) > 0.5


def put_exact_columns(mask, fetch, dual, sums_out):
    for p in range(WINDOW):

        @pl.when(is_listed(mask, p))
        def _(p=p):
            sums_out[place(p), :] = exact_columns(*fetch(p), dual)


def note_range(good, total):
    inside = jnp.logical_and(total >= SAFE_ROW, total <= HIGH_ROW)
    good[...] = jnp.minimum(good[...], jnp.where(inside, 1.0, 0.0))


def put_exact_rows(mask, fetch, bias, dual, total):
    count = dual.shape[0]

    def value(block, p, here):
        rows, target = block
        shift = jnp.where(is_listed(mask, p), bias[p : p + 1, :], NEG)
        return dot_nt(rows[here, :], target[...]) * TWO_KAPPA + shift

    dual[...] = jnp.full(dual.shape, NEG, jnp.float32)
    for p in range(WINDOW):
        block = fetch(p)

        def find(r, carry, p=p, block=block):
            here = pl.ds(pl.multiple_of(r * LANES, LANES), LANES)
            best = jnp.max(value(block, p, here), axis=1, keepdims=True)
            dual[here, :] = jnp.maximum(dual[here, :], best)
            return carry

        lax.fori_loop(0, count // LANES, find, 0)
    total[...] = jnp.zeros(total.shape, jnp.float32)
    for p in range(WINDOW):
        block = fetch(p)

        def add(r, carry, p=p, block=block):
            here = pl.ds(pl.multiple_of(r * LANES, LANES), LANES)
            e = jnp.exp2(value(block, p, here) - dual[here, 0:1])
            total[here, :] += jnp.sum(e, axis=1, keepdims=True)
            return carry

        lax.fori_loop(0, count // LANES, add, 0)
    dual[...] = -(dual[...] + jnp.log2(total[...]))


def add_columns(entries, here, scale, col, width):
    for q in range(width):
        e = entries[here, q * LANES : (q + 1) * LANES] * scale
        col[:, q * LANES : (q + 1) * LANES] += jnp.sum(e.reshape(LANES // 8, 8, LANES), axis=0)


def first_kernel(mask, rows, t0, t1, t2, t3, t4, entries, sums_out, top_out, base, dual, mass, good, col):
    targets = (t0, t1, t2, t3, t4)
    count = rows.shape[0]
    base[...] = jnp.zeros(base.shape, jnp.float32)
    for p in range(WINDOW):
        sq = jnp.square(targets[p][...].astype(jnp.float32))
        sq = sum(sq[:, q * LANES : (q + 1) * LANES] for q in range(sq.shape[1] // LANES))
        bias = jnp.concatenate(
            [
                jnp.sum(sq[r * LANES : (r + 1) * LANES, :].T, axis=0, keepdims=True)
                for r in range(count // LANES)
            ],
            axis=1,
        )
        bias = jnp.where(is_listed(mask, p), -KAPPA * bias, NEG)
        base[p : p + 1, :] = bias

    block = dot_nt(rows[...], targets[0][...]) * TWO_KAPPA + base[0:1, :]
    entries[:, 0:count] = block
    best = block[:, 0:LANES]
    for q in range(1, count // LANES):
        best = jnp.maximum(best, block[:, q * LANES : (q + 1) * LANES])
    top_out[...] = jnp.broadcast_to(jnp.max(best, axis=1, keepdims=True), (count, LANES))
    for p in (1, 2, 3, 4, 0):
        if p:
            block = dot_nt(rows[...], targets[p][...]) * TWO_KAPPA + base[p : p + 1, :]
        else:
            block = entries[:, 0:count]
        acc = jnp.zeros((count, LANES), jnp.float32) if p == 1 else mass[...]
        top = top_out[...]
        for q in range(count // LANES):
            e = jnp.exp2(block[:, q * LANES : (q + 1) * LANES] - top)
            entries[:, p * count + q * LANES : p * count + (q + 1) * LANES] = e
            acc = acc + e
        mass[...] = acc

    col[...] = jnp.zeros(col.shape, jnp.float32)
    good[...] = jnp.ones(good.shape, jnp.float32)
    width = WINDOW * count // LANES

    def rows_of(r):
        return pl.ds(pl.multiple_of(r * LANES, LANES), LANES)

    def invert(r, carry):
        here = rows_of(r)
        total = jnp.broadcast_to(jnp.sum(mass[here, :], axis=1, keepdims=True), (LANES, LANES))
        note_range(good, total)
        dual[here, :] = -(top_out[here, :] + jnp.log2(total))
        mass[here, :] = 1.0 / total
        return carry

    lax.fori_loop(0, count // LANES, invert, 0)

    def columns(r, carry):
        add_columns(entries, rows_of(r), mass[rows_of(r), :], col, width)
        return carry

    lax.fori_loop(0, count // LANES, columns, 0)
    fine = put_columns(mask, base, col, sums_out, jnp.min(good[...], axis=0, keepdims=True))

    @pl.when(jnp.logical_not(fine))
    def _():
        def fetch(p):
            return rows, targets[p]

        put_exact_rows(mask, fetch, base, dual, mass)
        put_exact_columns(mask, fetch, dual, sums_out)


def later_kernel(
    mask, entries, pot, base, top, rows_far, t0, t1, t2, t3, t4, sums_out, dual_out, gain, col, good, total, rows, target
):
    targets = (t0, t1, t2, t3, t4)
    count = rows.shape[0]

    def fetch(p):
        pltpu.sync_copy(rows_far, rows)
        pltpu.sync_copy(targets[p], target)
        return rows, target

    col[...] = jnp.zeros(col.shape, jnp.float32)
    width = WINDOW * count // LANES
    worst = jnp.zeros((1, count), jnp.float32)
    for p in range(WINDOW):
        taken = is_listed(mask, p)
        shift = jnp.where(taken, pot[p : p + 1, :] - base[p : p + 1, :], 0.0)
        worst = jnp.maximum(worst, jnp.abs(shift))
        gain[:, p * count : (p + 1) * count] = jnp.broadcast_to(
            jnp.where(taken, jnp.exp2(shift), 0.0), (8, count)
        )
    good[...] = jnp.ones(good.shape, jnp.float32)

    def rows_of(r):
        return pl.ds(pl.multiple_of(r * LANES, LANES), LANES)

    def weigh(r, meanwhile):
        here = rows_of(r)
        acc = jnp.zeros((LANES, LANES), jnp.float32)
        for q in range(width):
            at = slice(q * LANES, (q + 1) * LANES)
            acc = acc + entries[here, at] * gain[0:1, at]
        mass = jnp.broadcast_to(jnp.sum(acc, axis=1, keepdims=True), (LANES, LANES))
        meanwhile()
        note_range(good, mass)
        dual_out[here, :] = -(top[here, :] + jnp.log2(mass))
        total[here, :] = 1.0 / mass

    def columns(r):
        add_columns(entries, rows_of(r), total[rows_of(r), :], col, width)

    def both(r, carry):
        weigh(r, lambda: columns(r - 1))
        return carry

    weigh(0, lambda: None)
    lax.fori_loop(1, count // LANES, both, 0)
    columns(count // LANES - 1)
    fine = jnp.min(good[...], axis=0, keepdims=True)
    for q in range(count // LANES):
        fine = jnp.minimum(fine, jnp.where(worst[:, q * LANES : (q + 1) * LANES] <= SAFE_SHIFT, 1.0, 0.0))
    fine = put_columns(mask, base, col, sums_out, fine)

    @pl.when(jnp.logical_not(fine))
    def _():
        put_exact_rows(mask, fetch, pot, dual_out, total)
        put_exact_columns(mask, fetch, dual_out, sums_out)

    for r in range(count // LANES):
        here = slice(r * LANES, (r + 1) * LANES)
        sums_out[6:7, here] = dual_out[here, :].T[0:1, :]
    lane = lax.broadcasted_iota(jnp.int32, (1, LANES), 1)
    pairs = jnp.zeros((1, LANES), jnp.float32)
    for k in range(WINDOW):
        pairs = jnp.where(lane == k, mask[0, k].astype(jnp.float32), pairs)
    sums_out[7:8, 0:LANES] = pairs


VMEM = pl.BlockSpec(memory_space=pltpu.VMEM)
ANY = pl.BlockSpec(memory_space=pl.ANY)
SMEM = pl.BlockSpec(memory_space=pltpu.SMEM)


def first_step(mask, rows, targets):
    count, width = rows.shape
    pairs = WINDOW * count * count
    row = jax.ShapeDtypeStruct((8, count), jnp.float32)
    column = jax.ShapeDtypeStruct((count, LANES), jnp.float32)
    return pl.pallas_call(
        first_kernel,
        out_shape=(pltpu.VMEM((count, WINDOW * count), jnp.float32), row, column, row),
        in_specs=[SMEM] + [VMEM] * 6,
        out_specs=(VMEM,) * 4,
        scratch_shapes=[
            pltpu.VMEM((count, LANES), jnp.float32),
            pltpu.VMEM((count, LANES), jnp.float32),
            pltpu.VMEM((LANES, LANES), jnp.float32),
            pltpu.VMEM((8, WINDOW * count), jnp.float32),
        ],
        compiler_params=pltpu.CompilerParams(vmem_limit_bytes=SCOPED),
        cost_estimate=pl.CostEstimate(
            flops=2 * pairs * width, bytes_accessed=12 * count * width, transcendentals=pairs
        ),
        name="first_step",
    )(mask, rows, *targets)


def later_step(last, mask, entries, pot, base, top, rows, targets):
    count, width = rows.shape
    pairs = WINDOW * count * count
    row = jax.ShapeDtypeStruct((8, count), jnp.float32)
    column = jax.ShapeDtypeStruct((count, LANES), jnp.float32)
    entries = pltpu.with_memory_space_constraint(entries, pltpu.VMEM)
    out_shape = (row, column) if last else (row,)
    dual = [] if last else [pltpu.VMEM((count, LANES), jnp.float32)]
    return pl.pallas_call(
        later_kernel,
        out_shape=out_shape,
        in_specs=[SMEM] + [VMEM] * 4 + [ANY] * 6,
        out_specs=(VMEM,) * len(out_shape),
        scratch_shapes=dual
        + [
            pltpu.VMEM((8, WINDOW * count), jnp.float32),
            pltpu.VMEM((8, WINDOW * count), jnp.float32),
            pltpu.VMEM((LANES, LANES), jnp.float32),
            pltpu.VMEM((count, LANES), jnp.float32),
            pltpu.VMEM((count, width), jnp.bfloat16),
            pltpu.VMEM((count, width), jnp.bfloat16),
        ],
        compiler_params=pltpu.CompilerParams(vmem_limit_bytes=SCOPED),
        cost_estimate=pl.CostEstimate(
            flops=4 * pairs, bytes_accessed=12 * count * width, transcendentals=0
        ),
        name="later_step",
    )(mask, entries, pot, base, top, rows, *targets)


def grad_kernel(
    mask, pot, dual, around, mine, own, t0, t1, t2, t3, t4, x0, x1, x2, x3, x4, source_out, target_out
):
    targets = (t0, t1, t2, t3, t4)
    sources = (x0, x1, x2, x3, x4)
    width = own.shape[1]
    here = pl.ds(pl.multiple_of(lax.axis_index("grp") * LANES, LANES), LANES)
    dual_column = dual[here, 0:1]
    mass = jnp.zeros((LANES, 1), jnp.float32)
    carried = jnp.zeros((LANES, width), jnp.float32)
    for p in range(WINDOW):
        bias = jnp.where(is_listed(mask, p), pot[p : p + 1, :], NEG)
        weight = jnp.exp2(dot_nt(mine[...], targets[p][...]) * TWO_KAPPA + (dual_column + bias))
        weight = weight.astype(jnp.bfloat16)
        mass = mass + jnp.sum(weight.astype(jnp.float32), axis=1, keepdims=True)
        carried = carried + jnp.dot(weight, targets[p][...], preferred_element_type=jnp.float32)
    source_out[...] = 2.0 * (mine[...].astype(jnp.float32) * mass - carried)

    bias = jnp.broadcast_to(pot[0:1, here], (LANES, LANES)).T[:, 0:1]
    lane = lax.broadcasted_iota(jnp.int32, (1, LANES), 1)
    mass = jnp.zeros((LANES, 1), jnp.float32)
    pulled = jnp.zeros((LANES, width), jnp.float32)
    for p in range(WINDOW):
        low, high = ((2, 2), (1, 3), (3, 1), (0, 0), (4, 4))[p]
        slot = jnp.where(is_even(), low, high)
        taken = jnp.max(jnp.where(lane == slot, around[p, 1:2, 0:LANES], 0.0), axis=1, keepdims=True)
        shift = jnp.where(taken > 0.5, around[p, 0:1, :], NEG) + bias
        weight = jnp.exp2(dot_nt(own[...], sources[p][...]) * TWO_KAPPA + shift)
        weight = weight.astype(jnp.bfloat16)
        mass = mass + jnp.sum(weight.astype(jnp.float32), axis=1, keepdims=True)
        pulled = pulled + jnp.dot(weight, sources[p][...], preferred_element_type=jnp.float32)
    target_out[...] = 2.0 * (own[...].astype(jnp.float32) * mass - pulled)


def gradients(mask, pot, dual, around, mine, own, targets, sources):
    width = mine.shape[1]
    count = sources[0].shape[0]
    part = jax.ShapeDtypeStruct((LANES, width), jnp.float32)
    pairs = 2 * WINDOW * count * LANES
    return pl.pallas_call(
        grad_kernel,
        out_shape=(part, part),
        in_specs=[SMEM] + [VMEM] * 15,
        out_specs=(VMEM, VMEM),
        compiler_params=pltpu.CompilerParams(vmem_limit_bytes=SCOPED),
        cost_estimate=pl.CostEstimate(
            flops=4 * pairs * width, bytes_accessed=20 * count * width, transcendentals=pairs
        ),
        name="plan_gradients",
    )(mask, pot, dual, around, mine, own, *targets, *sources)


def neighbours(block, even):
    above = shifted(block, -2)
    below = shifted(block, 2)
    mate = swap_mate(block)
    cross = swap_mate(jnp.where(even, above, below))
    return block, mate, cross, above, below


def shards(source, target, pair_mask):
    row = lax.axis_index("row")
    even = row % 2 == 0
    up = (row // 2) // (1 + row % 2) % 2 == 0
    targets = neighbours(gathered(target), even)
    rows = gathered(source)
    rows, even, up = lax.optimization_barrier((rows, even, up))
    entries, partial, top, base = first_step(pair_mask, rows, targets)
    total, (above, below) = column_totals(
        partial, even, up, False, (rows,), (lambda x: shifted(x, -2), lambda x: shifted(x, 2)), True
    )
    (partial,) = later_step(False, pair_mask, entries, -total, base, top, rows, targets)
    total, (mate, cross) = column_totals(
        partial,
        even,
        up,
        False,
        (rows, above, below),
        (lambda x, a, b: swap_mate(x), lambda x, a, b: swap_mate(jnp.where(even, a, b))),
    )
    partial, dual = later_step(True, pair_mask, entries, -total, base, top, rows, targets)
    total, around = column_totals(partial, even, up, True)
    sources = (rows, mate, cross, above, below)
    return gradients(pair_mask, -total, dual, around, source, target, targets, sources)


def solution(mesh):
    placed = (P(("row", "grp"), None), P(("row", "grp"), None), P("row", None))
    return jax.shard_map(
        shards,
        mesh=mesh,
        in_specs=placed,
        out_specs=(P(("row", "grp"), None), P(("row", "grp"), None)),
        check_vma=False,
    )
```

```python
import functools
import math

import jax
import jax.numpy as jnp
from jax import lax
from jax.experimental import pallas as pl
from jax.experimental.pallas import tpu as pltpu
from jax.sharding import PartitionSpec as P

EPS = 0.1
NEG = -1e30
KAPPA = 1.0 / (EPS * math.log(2.0))
TWO_KAPPA = 2.0 * KAPPA
SAFE_SUM = 2.0 ** -60
SAFE_ROW = 2.0 ** -28
HIGH_ROW = 2.0 ** 60
SAFE_SHIFT = 60.0
SCOPED = 16 * 1024 * 1024
LANES = 128
WINDOW = 5


def from_row(block, source_of):
    count = lax.axis_size("row")
    return lax.ppermute(block, "row", [(source_of(i), i) for i in range(count)])


def swap_mate(block):
    return from_row(block, lambda i: i ^ 1)


def shifted(block, distance):
    count = lax.axis_size("row")
    return from_row(block, lambda i: (i - distance) % count)


def swap_chips(block, second):
    count = lax.axis_size("row")

    def source_of(i):
        chip, core = divmod(i, 2)
        reach = 1 + core
        up = (chip // reach) % 2 == 0
        if second:
            up = not up
        return (i + 2 * reach if up else i - 2 * reach) % count

    return from_row(block, source_of)


def gathered(shard):
    count = lax.axis_size("grp")
    copies = jnp.broadcast_to(shard[None], (count,) + shard.shape)
    return lax.all_to_all(copies, "grp", 0, 0, tiled=True).reshape(-1, shard.shape[1])


def lse2(a, b):
    top = jnp.maximum(a, b)
    return top + jnp.log2(jnp.exp2(a - top) + jnp.exp2(b - top))


def column_totals(partial, even, up, extra=False, cargo=None, movers=(), landed=None):
    count = 2 if extra else 0
    other = swap_mate(partial[: 6 + count])
    chip = lse2(partial[:6], other[:6])
    if landed is not None:
        chip, landed = lax.optimization_barrier((chip, landed))
    if movers:
        chip, cargo = lax.optimization_barrier((chip, cargo))
    to_above, to_below = chip[2:6], chip[0:4]
    if count:
        mine = partial[6:8]
        here = jnp.where(
            even, jnp.concatenate([mine, other[6:]]), jnp.concatenate([other[6:], mine])
        )
        to_above = jnp.concatenate([to_above, here])
        to_below = jnp.concatenate([to_below, here])
    one = swap_chips(jnp.where(up, to_above, to_below), False)
    two = swap_chips(jnp.where(up, to_below, to_above), True)
    above = jnp.where(up, one, two)
    below = jnp.where(up, two, one)
    blank = jnp.full_like(above[0:2], NEG)
    outer = jnp.where(
        even,
        jnp.concatenate([below[0:2], lse2(below[2:4], above[0:2]), above[2:4]]),
        jnp.concatenate([below[2:4], blank, above[0:2]]),
    )
    sent = jnp.concatenate([outer, below[4:], above[4:]]) if count else outer
    got = swap_mate(sent)
    total = lse2(chip, lse2(outer, got[:6]))
    if movers:
        moved = [move(*cargo) for move in movers]
        total, moved = lax.optimization_barrier((total, moved))

    def placed(rows):
        return jnp.where(
            even,
            jnp.stack([rows[2], rows[3], rows[1], rows[4], rows[0]]),
            jnp.stack([rows[3], rows[2], rows[4], rows[5], rows[1]]),
        )

    if movers:
        return placed(total), moved
    if landed is not None:
        return placed(total), landed
    if not count:
        return placed(total)
    near = jnp.where(even, sent[6:], got[6:])
    around = jnp.concatenate([near[:4], here, near[4:]]).reshape(6, count, -1)
    return placed(total), placed(around)


def dot_nt(a, b):
    return lax.dot_general(a, b, (((1,), (1,)), ((), ())), preferred_element_type=jnp.float32)


def exact_columns(rows, target, dual):
    count = rows.shape[0]

    def value(r):
        here = pl.ds(pl.multiple_of(r * LANES, LANES), LANES)
        return dot_nt(rows[here, :], target[...]) * TWO_KAPPA + dual[here, 0:1]

    def find(r, best):
        return jnp.maximum(best, jnp.max(value(r), axis=0, keepdims=True))

    best = lax.fori_loop(0, count // LANES, find, jnp.full((1, count), NEG, jnp.float32))

    def add(r, acc):
        return acc + jnp.sum(jnp.exp2(value(r) - best), axis=0, keepdims=True)

    acc = lax.fori_loop(0, count // LANES, add, jnp.zeros((1, count), jnp.float32))
    return best + jnp.log2(acc)


def is_even():
    return lax.rem(lax.axis_index("row"), 2) == 0


def place(p):
    low, high = ((2, 3), (3, 2), (1, 4), (4, 5), (0, 1))[p]
    return pl.ds(jnp.where(is_even(), low, high), 1)


def is_listed(mask, p):
    low, high = ((2, 2), (3, 1), (1, 3), (4, 4), (0, 0))[p]
    return mask[0, jnp.where(is_even(), low, high)] == 1


def put_columns(mask, base, col, sums_out, fine):
    count = sums_out.shape[1]
    sums_out[...] = jnp.full(sums_out.shape, NEG, jnp.float32)
    for p in range(WINDOW):
        sums = jnp.sum(col[:, p * count : (p + 1) * count], axis=0, keepdims=True)
        taken = is_listed(mask, p)
        sums_out[place(p), :] = jnp.where(taken, jnp.log2(sums) - base[p : p + 1, :], NEG)
        good = jnp.where(jnp.logical_or(jnp.logical_not(taken), sums >= SAFE_SUM), 1.0, 0.0)
        for q in range(count // LANES):
            fine = jnp.minimum(fine, good[:, q * LANES : (q + 1) * LANES])
    return jnp.min(fine) > 0.5


def put_exact_columns(mask, fetch, dual, sums_out):
    for p in range(WINDOW):

        @pl.when(is_listed(mask, p))
        def _(p=p):
            sums_out[place(p), :] = exact_columns(*fetch(p), dual)


def note_range(good, total):
    inside = jnp.logical_and(total >= SAFE_ROW, total <= HIGH_ROW)
    good[...] = jnp.minimum(good[...], jnp.where(inside, 1.0, 0.0))


def put_exact_rows(mask, fetch, bias, dual, total):
    count = dual.shape[0]

    def value(block, p, here):
        rows, target = block
        shift = jnp.where(is_listed(mask, p), bias[p : p + 1, :], NEG)
        return dot_nt(rows[here, :], target[...]) * TWO_KAPPA + shift

    dual[...] = jnp.full(dual.shape, NEG, jnp.float32)
    for p in range(WINDOW):
        block = fetch(p)

        def find(r, carry, p=p, block=block):
            here = pl.ds(pl.multiple_of(r * LANES, LANES), LANES)
            best = jnp.max(value(block, p, here), axis=1, keepdims=True)
            dual[here, :] = jnp.maximum(dual[here, :], best)
            return carry

        lax.fori_loop(0, count // LANES, find, 0)
    total[...] = jnp.zeros(total.shape, jnp.float32)
    for p in range(WINDOW):
        block = fetch(p)

        def add(r, carry, p=p, block=block):
            here = pl.ds(pl.multiple_of(r * LANES, LANES), LANES)
            e = jnp.exp2(value(block, p, here) - dual[here, 0:1])
            total[here, :] += jnp.sum(e, axis=1, keepdims=True)
            return carry

        lax.fori_loop(0, count // LANES, add, 0)
    dual[...] = -(dual[...] + jnp.log2(total[...]))


def add_columns(entries, here, scale, col, width):
    for q in range(width):
        e = entries[here, q * LANES : (q + 1) * LANES] * scale
        col[:, q * LANES : (q + 1) * LANES] += jnp.sum(e.reshape(LANES // 8, 8, LANES), axis=0)


def first_kernel(mask, rows, t0, t1, t2, t3, t4, entries, sums_out, top_out, base, dual, mass, good, col):
    targets = (t0, t1, t2, t3, t4)
    count = rows.shape[0]
    base[...] = jnp.zeros(base.shape, jnp.float32)
    for p in range(WINDOW):
        sq = jnp.square(targets[p][...].astype(jnp.float32))
        sq = sum(sq[:, q * LANES : (q + 1) * LANES] for q in range(sq.shape[1] // LANES))
        bias = jnp.concatenate(
            [
                jnp.sum(sq[r * LANES : (r + 1) * LANES, :].T, axis=0, keepdims=True)
                for r in range(count // LANES)
            ],
            axis=1,
        )
        bias = jnp.where(is_listed(mask, p), -KAPPA * bias, NEG)
        base[p : p + 1, :] = bias

    block = dot_nt(rows[...], targets[0][...]) * TWO_KAPPA + base[0:1, :]
    entries[:, 0:count] = block
    best = block[:, 0:LANES]
    for q in range(1, count // LANES):
        best = jnp.maximum(best, block[:, q * LANES : (q + 1) * LANES])
    top_out[...] = jnp.broadcast_to(jnp.max(best, axis=1, keepdims=True), (count, LANES))
    for p in (1, 2, 3, 4, 0):
        if p:
            block = dot_nt(rows[...], targets[p][...]) * TWO_KAPPA + base[p : p + 1, :]
        else:
            block = entries[:, 0:count]
        acc = jnp.zeros((count, LANES), jnp.float32) if p == 1 else mass[...]
        top = top_out[...]
        for q in range(count // LANES):
            e = jnp.exp2(block[:, q * LANES : (q + 1) * LANES] - top)
            entries[:, p * count + q * LANES : p * count + (q + 1) * LANES] = e
            acc = acc + e
        mass[...] = acc

    col[...] = jnp.zeros(col.shape, jnp.float32)
    good[...] = jnp.ones(good.shape, jnp.float32)
    width = WINDOW * count // LANES

    def rows_of(r):
        return pl.ds(pl.multiple_of(r * LANES, LANES), LANES)

    def invert(r, carry):
        here = rows_of(r)
        total = jnp.broadcast_to(jnp.sum(mass[here, :], axis=1, keepdims=True), (LANES, LANES))
        note_range(good, total)
        dual[here, :] = -(top_out[here, :] + jnp.log2(total))
        mass[here, :] = 1.0 / total
        return carry

    lax.fori_loop(0, count // LANES, invert, 0)

    def columns(r, carry):
        add_columns(entries, rows_of(r), mass[rows_of(r), :], col, width)
        return carry

    lax.fori_loop(0, count // LANES, columns, 0)
    fine = put_columns(mask, base, col, sums_out, jnp.min(good[...], axis=0, keepdims=True))

    @pl.when(jnp.logical_not(fine))
    def _():
        def fetch(p):
            return rows, targets[p]

        put_exact_rows(mask, fetch, base, dual, mass)
        put_exact_columns(mask, fetch, dual, sums_out)


def later_kernel(
    mask, entries, pot, base, top, rows_far, t0, t1, t2, t3, t4, sums_out, dual_out, gain, col, good, total, rows, target
):
    targets = (t0, t1, t2, t3, t4)
    count = rows.shape[0]

    def fetch(p):
        pltpu.sync_copy(rows_far, rows)
        pltpu.sync_copy(targets[p], target)
        return rows, target

    col[...] = jnp.zeros(col.shape, jnp.float32)
    width = WINDOW * count // LANES
    worst = jnp.zeros((1, count), jnp.float32)
    for p in range(WINDOW):
        taken = is_listed(mask, p)
        shift = jnp.where(taken, pot[p : p + 1, :] - base[p : p + 1, :], 0.0)
        worst = jnp.maximum(worst, jnp.abs(shift))
        gain[:, p * count : (p + 1) * count] = jnp.broadcast_to(
            jnp.where(taken, jnp.exp2(shift), 0.0), (8, count)
        )
    good[...] = jnp.ones(good.shape, jnp.float32)

    def rows_of(r):
        return pl.ds(pl.multiple_of(r * LANES, LANES), LANES)

    def weigh(r, meanwhile):
        here = rows_of(r)
        acc = jnp.zeros((LANES, LANES), jnp.float32)
        for q in range(width):
            at = slice(q * LANES, (q + 1) * LANES)
            acc = acc + entries[here, at] * gain[0:1, at]
        mass = jnp.broadcast_to(jnp.sum(acc, axis=1, keepdims=True), (LANES, LANES))
        meanwhile()
        note_range(good, mass)
        dual_out[here, :] = -(top[here, :] + jnp.log2(mass))
        total[here, :] = 1.0 / mass

    def columns(r):
        add_columns(entries, rows_of(r), total[rows_of(r), :], col, width)

    def both(r, carry):
        weigh(r, lambda: columns(r - 1))
        return carry

    weigh(0, lambda: None)
    lax.fori_loop(1, count // LANES, both, 0)
    columns(count // LANES - 1)
    fine = jnp.min(good[...], axis=0, keepdims=True)
    for q in range(count // LANES):
        fine = jnp.minimum(fine, jnp.where(worst[:, q * LANES : (q + 1) * LANES] <= SAFE_SHIFT, 1.0, 0.0))
    fine = put_columns(mask, base, col, sums_out, fine)

    @pl.when(jnp.logical_not(fine))
    def _():
        put_exact_rows(mask, fetch, pot, dual_out, total)
        put_exact_columns(mask, fetch, dual_out, sums_out)

    for r in range(count // LANES):
        here = slice(r * LANES, (r + 1) * LANES)
        sums_out[6:7, here] = dual_out[here, :].T[0:1, :]
    lane = lax.broadcasted_iota(jnp.int32, (1, LANES), 1)
    pairs = jnp.zeros((1, LANES), jnp.float32)
    for k in range(WINDOW):
        pairs = jnp.where(lane == k, mask[0, k].astype(jnp.float32), pairs)
    sums_out[7:8, 0:LANES] = pairs


VMEM = pl.BlockSpec(memory_space=pltpu.VMEM)
ANY = pl.BlockSpec(memory_space=pl.ANY)
SMEM = pl.BlockSpec(memory_space=pltpu.SMEM)


def first_step(mask, rows, targets):
    count, width = rows.shape
    pairs = WINDOW * count * count
    row = jax.ShapeDtypeStruct((8, count), jnp.float32)
    column = jax.ShapeDtypeStruct((count, LANES), jnp.float32)
    return pl.pallas_call(
        first_kernel,
        out_shape=(pltpu.VMEM((count, WINDOW * count), jnp.float32), row, column, row),
        in_specs=[SMEM] + [VMEM] * 6,
        out_specs=(VMEM,) * 4,
        scratch_shapes=[
            pltpu.VMEM((count, LANES), jnp.float32),
            pltpu.VMEM((count, LANES), jnp.float32),
            pltpu.VMEM((LANES, LANES), jnp.float32),
            pltpu.VMEM((8, WINDOW * count), jnp.float32),
        ],
        compiler_params=pltpu.CompilerParams(vmem_limit_bytes=SCOPED),
        cost_estimate=pl.CostEstimate(
            flops=2 * pairs * width, bytes_accessed=12 * count * width, transcendentals=pairs
        ),
        name="first_step",
    )(mask, rows, *targets)


def later_step(last, mask, entries, pot, base, top, rows, targets):
    count, width = rows.shape
    pairs = WINDOW * count * count
    row = jax.ShapeDtypeStruct((8, count), jnp.float32)
    column = jax.ShapeDtypeStruct((count, LANES), jnp.float32)
    entries = pltpu.with_memory_space_constraint(entries, pltpu.VMEM)
    out_shape = (row, column) if last else (row,)
    dual = [] if last else [pltpu.VMEM((count, LANES), jnp.float32)]
    return pl.pallas_call(
        later_kernel,
        out_shape=out_shape,
        in_specs=[SMEM] + [VMEM] * 4 + [ANY] * 6,
        out_specs=(VMEM,) * len(out_shape),
        scratch_shapes=dual
        + [
            pltpu.VMEM((8, WINDOW * count), jnp.float32),
            pltpu.VMEM((8, WINDOW * count), jnp.float32),
            pltpu.VMEM((LANES, LANES), jnp.float32),
            pltpu.VMEM((count, LANES), jnp.float32),
            pltpu.VMEM((count, width), jnp.bfloat16),
            pltpu.VMEM((count, width), jnp.bfloat16),
        ],
        compiler_params=pltpu.CompilerParams(vmem_limit_bytes=SCOPED),
        cost_estimate=pl.CostEstimate(
            flops=4 * pairs, bytes_accessed=12 * count * width, transcendentals=0
        ),
        name="later_step",
    )(mask, entries, pot, base, top, rows, *targets)


def grad_kernel(
    mask, pot, dual, around, mine, own, t0, t1, t2, t3, t4, x0, x1, x2, x3, x4, source_out, target_out
):
    targets = (t0, t1, t2, t3, t4)
    sources = (x0, x1, x2, x3, x4)
    width = own.shape[1]
    here = pl.ds(pl.multiple_of(lax.axis_index("grp") * LANES, LANES), LANES)
    dual_column = dual[here, 0:1]
    mass = jnp.zeros((LANES, 1), jnp.float32)
    carried = jnp.zeros((LANES, width), jnp.float32)
    for p in range(WINDOW):
        bias = jnp.where(is_listed(mask, p), pot[p : p + 1, :], NEG)
        weight = jnp.exp2(dot_nt(mine[...], targets[p][...]) * TWO_KAPPA + (dual_column + bias))
        weight = weight.astype(jnp.bfloat16)
        mass = mass + jnp.sum(weight.astype(jnp.float32), axis=1, keepdims=True)
        carried = carried + jnp.dot(weight, targets[p][...], preferred_element_type=jnp.float32)
    source_out[...] = 2.0 * (mine[...].astype(jnp.float32) * mass - carried)

    bias = jnp.broadcast_to(pot[0:1, here], (LANES, LANES)).T[:, 0:1]
    lane = lax.broadcasted_iota(jnp.int32, (1, LANES), 1)
    mass = jnp.zeros((LANES, 1), jnp.float32)
    pulled = jnp.zeros((LANES, width), jnp.float32)
    for p in range(WINDOW):
        low, high = ((2, 2), (1, 3), (3, 1), (0, 0), (4, 4))[p]
        slot = jnp.where(is_even(), low, high)
        taken = jnp.max(jnp.where(lane == slot, around[p, 1:2, 0:LANES], 0.0), axis=1, keepdims=True)
        shift = jnp.where(taken > 0.5, around[p, 0:1, :], NEG) + bias
        weight = jnp.exp2(dot_nt(own[...], sources[p][...]) * TWO_KAPPA + shift)
        weight = weight.astype(jnp.bfloat16)
        mass = mass + jnp.sum(weight.astype(jnp.float32), axis=1, keepdims=True)
        pulled = pulled + jnp.dot(weight, sources[p][...], preferred_element_type=jnp.float32)
    target_out[...] = 2.0 * (own[...].astype(jnp.float32) * mass - pulled)


def gradients(mask, pot, dual, around, mine, own, targets, sources):
    width = mine.shape[1]
    count = sources[0].shape[0]
    part = jax.ShapeDtypeStruct((LANES, width), jnp.float32)
    pairs = 2 * WINDOW * count * LANES
    return pl.pallas_call(
        grad_kernel,
        out_shape=(part, part),
        in_specs=[SMEM] + [VMEM] * 15,
        out_specs=(VMEM, VMEM),
        compiler_params=pltpu.CompilerParams(vmem_limit_bytes=SCOPED),
        cost_estimate=pl.CostEstimate(
            flops=4 * pairs * width, bytes_accessed=20 * count * width, transcendentals=pairs
        ),
        name="plan_gradients",
    )(mask, pot, dual, around, mine, own, *targets, *sources)


def neighbours(block, even):
    above = shifted(block, -2)
    below = shifted(block, 2)
    mate = swap_mate(block)
    cross = swap_mate(jnp.where(even, above, below))
    return block, mate, cross, above, below


def shards(source, target, pair_mask):
    row = lax.axis_index("row")
    even = row % 2 == 0
    up = (row // 2) // (1 + row % 2) % 2 == 0
    targets = neighbours(gathered(target), even)
    rows = gathered(source)
    rows, even, up = lax.optimization_barrier((rows, even, up))
    entries, partial, top, base = first_step(pair_mask, rows, targets)
    total, (above, below) = column_totals(
        partial, even, up, landed=(shifted(rows, -2), shifted(rows, 2))
    )
    (partial,) = later_step(False, pair_mask, entries, -total, base, top, rows, targets)
    total, (mate, cross) = column_totals(
        partial,
        even,
        up,
        False,
        (rows, above, below),
        (lambda x, a, b: swap_mate(x), lambda x, a, b: swap_mate(jnp.where(even, a, b))),
    )
    partial, dual = later_step(True, pair_mask, entries, -total, base, top, rows, targets)
    total, around = column_totals(partial, even, up, True)
    sources = (rows, mate, cross, above, below)
    return gradients(pair_mask, -total, dual, around, source, target, targets, sources)


def solution(mesh):
    placed = (P(("row", "grp"), None), P(("row", "grp"), None), P("row", None))
    return jax.shard_map(
        shards,
        mesh=mesh,
        in_specs=placed,
        out_specs=(P(("row", "grp"), None), P(("row", "grp"), None)),
        check_vma=False,
    )
```

```python
import functools
import math

import jax
import jax.numpy as jnp
from jax import lax
from jax.experimental import pallas as pl
from jax.experimental.pallas import tpu as pltpu
from jax.sharding import PartitionSpec as P

EPS = 0.1
NEG = -1e30
KAPPA = 1.0 / (EPS * math.log(2.0))
TWO_KAPPA = 2.0 * KAPPA
SAFE_SUM = 2.0 ** -60
SAFE_ROW = 2.0 ** -28
HIGH_ROW = 2.0 ** 60
SAFE_SHIFT = 60.0
SCOPED = 16 * 1024 * 1024
LANES = 128
WINDOW = 5


def from_row(block, source_of):
    count = lax.axis_size("row")
    return lax.ppermute(block, "row", [(source_of(i), i) for i in range(count)])


def swap_mate(block):
    return from_row(block, lambda i: i ^ 1)


def shifted(block, distance):
    count = lax.axis_size("row")
    return from_row(block, lambda i: (i - distance) % count)


def swap_chips(block, second):
    count = lax.axis_size("row")

    def source_of(i):
        chip, core = divmod(i, 2)
        reach = 1 + core
        up = (chip // reach) % 2 == 0
        if second:
            up = not up
        return (i + 2 * reach if up else i - 2 * reach) % count

    return from_row(block, source_of)


def gathered(shard):
    count = lax.axis_size("grp")
    copies = jnp.broadcast_to(shard[None], (count,) + shard.shape)
    return lax.all_to_all(copies, "grp", 0, 0, tiled=True).reshape(-1, shard.shape[1])


def lse2(a, b):
    top = jnp.maximum(a, b)
    return top + jnp.log2(jnp.exp2(a - top) + jnp.exp2(b - top))


def column_totals(partial, even, up, extra=False, cargo=None, movers=(), landed=None):
    count = 2 if extra else 0
    other = swap_mate(partial[: 6 + count])
    chip = lse2(partial[:6], other[:6])
    if landed is not None:
        chip, landed = lax.optimization_barrier((chip, landed))
    if movers:
        chip, cargo = lax.optimization_barrier((chip, cargo))
    to_above, to_below = chip[2:6], chip[0:4]
    if count:
        mine = partial[6:8]
        here = jnp.where(
            even, jnp.concatenate([mine, other[6:]]), jnp.concatenate([other[6:], mine])
        )
        to_above = jnp.concatenate([to_above, here])
        to_below = jnp.concatenate([to_below, here])
    one = swap_chips(jnp.where(up, to_above, to_below), False)
    two = swap_chips(jnp.where(up, to_below, to_above), True)
    above = jnp.where(up, one, two)
    below = jnp.where(up, two, one)
    blank = jnp.full_like(above[0:2], NEG)
    outer = jnp.where(
        even,
        jnp.concatenate([below[0:2], lse2(below[2:4], above[0:2]), above[2:4]]),
        jnp.concatenate([below[2:4], blank, above[0:2]]),
    )
    sent = jnp.concatenate([outer, below[4:], above[4:]]) if count else outer
    got = swap_mate(sent)
    total = lse2(chip, lse2(outer, got[:6]))
    if movers:
        moved = [move(*cargo) for move in movers]
        total, moved = lax.optimization_barrier((total, moved))

    def placed(rows):
        return jnp.where(
            even,
            jnp.stack([rows[2], rows[3], rows[1], rows[4], rows[0]]),
            jnp.stack([rows[3], rows[2], rows[4], rows[5], rows[1]]),
        )

    if movers:
        return placed(total), moved + list(landed or ())
    if landed is not None:
        return placed(total), landed
    if not count:
        return placed(total)
    near = jnp.where(even, sent[6:], got[6:])
    around = jnp.concatenate([near[:4], here, near[4:]]).reshape(6, count, -1)
    return placed(total), placed(around)


def dot_nt(a, b):
    return lax.dot_general(a, b, (((1,), (1,)), ((), ())), preferred_element_type=jnp.float32)


def exact_columns(rows, target, dual):
    count = rows.shape[0]

    def value(r):
        here = pl.ds(pl.multiple_of(r * LANES, LANES), LANES)
        return dot_nt(rows[here, :], target[...]) * TWO_KAPPA + dual[here, 0:1]

    def find(r, best):
        return jnp.maximum(best, jnp.max(value(r), axis=0, keepdims=True))

    best = lax.fori_loop(0, count // LANES, find, jnp.full((1, count), NEG, jnp.float32))

    def add(r, acc):
        return acc + jnp.sum(jnp.exp2(value(r) - best), axis=0, keepdims=True)

    acc = lax.fori_loop(0, count // LANES, add, jnp.zeros((1, count), jnp.float32))
    return best + jnp.log2(acc)


def is_even():
    return lax.rem(lax.axis_index("row"), 2) == 0


def place(p):
    low, high = ((2, 3), (3, 2), (1, 4), (4, 5), (0, 1))[p]
    return pl.ds(jnp.where(is_even(), low, high), 1)


def is_listed(mask, p):
    low, high = ((2, 2), (3, 1), (1, 3), (4, 4), (0, 0))[p]
    return mask[0, jnp.where(is_even(), low, high)] == 1


def put_columns(mask, base, col, sums_out, fine):
    count = sums_out.shape[1]
    sums_out[...] = jnp.full(sums_out.shape, NEG, jnp.float32)
    for p in range(WINDOW):
        sums = jnp.sum(col[:, p * count : (p + 1) * count], axis=0, keepdims=True)
        taken = is_listed(mask, p)
        sums_out[place(p), :] = jnp.where(taken, jnp.log2(sums) - base[p : p + 1, :], NEG)
        good = jnp.where(jnp.logical_or(jnp.logical_not(taken), sums >= SAFE_SUM), 1.0, 0.0)
        for q in range(count // LANES):
            fine = jnp.minimum(fine, good[:, q * LANES : (q + 1) * LANES])
    return jnp.min(fine) > 0.5


def put_exact_columns(mask, fetch, dual, sums_out):
    for p in range(WINDOW):

        @pl.when(is_listed(mask, p))
        def _(p=p):
            sums_out[place(p), :] = exact_columns(*fetch(p), dual)


def note_range(good, total):
    inside = jnp.logical_and(total >= SAFE_ROW, total <= HIGH_ROW)
    good[...] = jnp.minimum(good[...], jnp.where(inside, 1.0, 0.0))


def put_exact_rows(mask, fetch, bias, dual, total):
    count = dual.shape[0]

    def value(block, p, here):
        rows, target = block
        shift = jnp.where(is_listed(mask, p), bias[p : p + 1, :], NEG)
        return dot_nt(rows[here, :], target[...]) * TWO_KAPPA + shift

    dual[...] = jnp.full(dual.shape, NEG, jnp.float32)
    for p in range(WINDOW):
        block = fetch(p)

        def find(r, carry, p=p, block=block):
            here = pl.ds(pl.multiple_of(r * LANES, LANES), LANES)
            best = jnp.max(value(block, p, here), axis=1, keepdims=True)
            dual[here, :] = jnp.maximum(dual[here, :], best)
            return carry

        lax.fori_loop(0, count // LANES, find, 0)
    total[...] = jnp.zeros(total.shape, jnp.float32)
    for p in range(WINDOW):
        block = fetch(p)

        def add(r, carry, p=p, block=block):
            here = pl.ds(pl.multiple_of(r * LANES, LANES), LANES)
            e = jnp.exp2(value(block, p, here) - dual[here, 0:1])
            total[here, :] += jnp.sum(e, axis=1, keepdims=True)
            return carry

        lax.fori_loop(0, count // LANES, add, 0)
    dual[...] = -(dual[...] + jnp.log2(total[...]))


def add_columns(entries, here, scale, col, width):
    for q in range(width):
        e = entries[here, q * LANES : (q + 1) * LANES] * scale
        col[:, q * LANES : (q + 1) * LANES] += jnp.sum(e.reshape(LANES // 8, 8, LANES), axis=0)


def first_kernel(mask, rows, t0, t1, t2, t3, t4, entries, sums_out, top_out, base, dual, mass, good, col):
    targets = (t0, t1, t2, t3, t4)
    count = rows.shape[0]
    base[...] = jnp.zeros(base.shape, jnp.float32)
    for p in range(WINDOW):
        sq = jnp.square(targets[p][...].astype(jnp.float32))
        sq = sum(sq[:, q * LANES : (q + 1) * LANES] for q in range(sq.shape[1] // LANES))
        bias = jnp.concatenate(
            [
                jnp.sum(sq[r * LANES : (r + 1) * LANES, :].T, axis=0, keepdims=True)
                for r in range(count // LANES)
            ],
            axis=1,
        )
        bias = jnp.where(is_listed(mask, p), -KAPPA * bias, NEG)
        base[p : p + 1, :] = bias

    block = dot_nt(rows[...], targets[0][...]) * TWO_KAPPA + base[0:1, :]
    entries[:, 0:count] = block
    best = block[:, 0:LANES]
    for q in range(1, count // LANES):
        best = jnp.maximum(best, block[:, q * LANES : (q + 1) * LANES])
    top_out[...] = jnp.broadcast_to(jnp.max(best, axis=1, keepdims=True), (count, LANES))
    for p in (1, 2, 3, 4, 0):
        if p:
            block = dot_nt(rows[...], targets[p][...]) * TWO_KAPPA + base[p : p + 1, :]
        else:
            block = entries[:, 0:count]
        acc = jnp.zeros((count, LANES), jnp.float32) if p == 1 else mass[...]
        top = top_out[...]
        for q in range(count // LANES):
            e = jnp.exp2(block[:, q * LANES : (q + 1) * LANES] - top)
            entries[:, p * count + q * LANES : p * count + (q + 1) * LANES] = e
            acc = acc + e
        mass[...] = acc

    col[...] = jnp.zeros(col.shape, jnp.float32)
    good[...] = jnp.ones(good.shape, jnp.float32)
    width = WINDOW * count // LANES

    def rows_of(r):
        return pl.ds(pl.multiple_of(r * LANES, LANES), LANES)

    def invert(r, carry):
        here = rows_of(r)
        total = jnp.broadcast_to(jnp.sum(mass[here, :], axis=1, keepdims=True), (LANES, LANES))
        note_range(good, total)
        dual[here, :] = -(top_out[here, :] + jnp.log2(total))
        mass[here, :] = 1.0 / total
        return carry

    lax.fori_loop(0, count // LANES, invert, 0)

    def columns(r, carry):
        add_columns(entries, rows_of(r), mass[rows_of(r), :], col, width)
        return carry

    lax.fori_loop(0, count // LANES, columns, 0)
    fine = put_columns(mask, base, col, sums_out, jnp.min(good[...], axis=0, keepdims=True))

    @pl.when(jnp.logical_not(fine))
    def _():
        def fetch(p):
            return rows, targets[p]

        put_exact_rows(mask, fetch, base, dual, mass)
        put_exact_columns(mask, fetch, dual, sums_out)


def later_kernel(
    mask, entries, pot, base, top, rows_far, t0, t1, t2, t3, t4, sums_out, dual_out, gain, col, good, total, rows, target
):
    targets = (t0, t1, t2, t3, t4)
    count = rows.shape[0]

    def fetch(p):
        pltpu.sync_copy(rows_far, rows)
        pltpu.sync_copy(targets[p], target)
        return rows, target

    col[...] = jnp.zeros(col.shape, jnp.float32)
    width = WINDOW * count // LANES
    worst = jnp.zeros((1, count), jnp.float32)
    for p in range(WINDOW):
        taken = is_listed(mask, p)
        shift = jnp.where(taken, pot[p : p + 1, :] - base[p : p + 1, :], 0.0)
        worst = jnp.maximum(worst, jnp.abs(shift))
        gain[:, p * count : (p + 1) * count] = jnp.broadcast_to(
            jnp.where(taken, jnp.exp2(shift), 0.0), (8, count)
        )
    good[...] = jnp.ones(good.shape, jnp.float32)

    def rows_of(r):
        return pl.ds(pl.multiple_of(r * LANES, LANES), LANES)

    def weigh(r, meanwhile):
        here = rows_of(r)
        acc = jnp.zeros((LANES, LANES), jnp.float32)
        for q in range(width):
            at = slice(q * LANES, (q + 1) * LANES)
            acc = acc + entries[here, at] * gain[0:1, at]
        mass = jnp.broadcast_to(jnp.sum(acc, axis=1, keepdims=True), (LANES, LANES))
        meanwhile()
        note_range(good, mass)
        dual_out[here, :] = -(top[here, :] + jnp.log2(mass))
        total[here, :] = 1.0 / mass

    def columns(r):
        add_columns(entries, rows_of(r), total[rows_of(r), :], col, width)

    def both(r, carry):
        weigh(r, lambda: columns(r - 1))
        return carry

    weigh(0, lambda: None)
    lax.fori_loop(1, count // LANES, both, 0)
    columns(count // LANES - 1)
    fine = jnp.min(good[...], axis=0, keepdims=True)
    for q in range(count // LANES):
        fine = jnp.minimum(fine, jnp.where(worst[:, q * LANES : (q + 1) * LANES] <= SAFE_SHIFT, 1.0, 0.0))
    fine = put_columns(mask, base, col, sums_out, fine)

    @pl.when(jnp.logical_not(fine))
    def _():
        put_exact_rows(mask, fetch, pot, dual_out, total)
        put_exact_columns(mask, fetch, dual_out, sums_out)

    for r in range(count // LANES):
        here = slice(r * LANES, (r + 1) * LANES)
        sums_out[6:7, here] = dual_out[here, :].T[0:1, :]
    lane = lax.broadcasted_iota(jnp.int32, (1, LANES), 1)
    pairs = jnp.zeros((1, LANES), jnp.float32)
    for k in range(WINDOW):
        pairs = jnp.where(lane == k, mask[0, k].astype(jnp.float32), pairs)
    sums_out[7:8, 0:LANES] = pairs


VMEM = pl.BlockSpec(memory_space=pltpu.VMEM)
ANY = pl.BlockSpec(memory_space=pl.ANY)
SMEM = pl.BlockSpec(memory_space=pltpu.SMEM)


def first_step(mask, rows, targets):
    count, width = rows.shape
    pairs = WINDOW * count * count
    row = jax.ShapeDtypeStruct((8, count), jnp.float32)
    column = jax.ShapeDtypeStruct((count, LANES), jnp.float32)
    return pl.pallas_call(
        first_kernel,
        out_shape=(pltpu.VMEM((count, WINDOW * count), jnp.float32), row, column, row),
        in_specs=[SMEM] + [VMEM] * 6,
        out_specs=(VMEM,) * 4,
        scratch_shapes=[
            pltpu.VMEM((count, LANES), jnp.float32),
            pltpu.VMEM((count, LANES), jnp.float32),
            pltpu.VMEM((LANES, LANES), jnp.float32),
            pltpu.VMEM((8, WINDOW * count), jnp.float32),
        ],
        compiler_params=pltpu.CompilerParams(vmem_limit_bytes=SCOPED),
        cost_estimate=pl.CostEstimate(
            flops=2 * pairs * width, bytes_accessed=12 * count * width, transcendentals=pairs
        ),
        name="first_step",
    )(mask, rows, *targets)


def later_step(last, mask, entries, pot, base, top, rows, targets):
    count, width = rows.shape
    pairs = WINDOW * count * count
    row = jax.ShapeDtypeStruct((8, count), jnp.float32)
    column = jax.ShapeDtypeStruct((count, LANES), jnp.float32)
    entries = pltpu.with_memory_space_constraint(entries, pltpu.VMEM)
    out_shape = (row, column) if last else (row,)
    dual = [] if last else [pltpu.VMEM((count, LANES), jnp.float32)]
    return pl.pallas_call(
        later_kernel,
        out_shape=out_shape,
        in_specs=[SMEM] + [VMEM] * 4 + [ANY] * 6,
        out_specs=(VMEM,) * len(out_shape),
        scratch_shapes=dual
        + [
            pltpu.VMEM((8, WINDOW * count), jnp.float32),
            pltpu.VMEM((8, WINDOW * count), jnp.float32),
            pltpu.VMEM((LANES, LANES), jnp.float32),
            pltpu.VMEM((count, LANES), jnp.float32),
            pltpu.VMEM((count, width), jnp.bfloat16),
            pltpu.VMEM((count, width), jnp.bfloat16),
        ],
        compiler_params=pltpu.CompilerParams(vmem_limit_bytes=SCOPED),
        cost_estimate=pl.CostEstimate(
            flops=4 * pairs, bytes_accessed=12 * count * width, transcendentals=0
        ),
        name="later_step",
    )(mask, entries, pot, base, top, rows, *targets)


def grad_kernel(
    mask, pot, dual, around, mine, own, t0, t1, t2, t3, t4, x0, x1, x2, x3, x4, source_out, target_out
):
    targets = (t0, t1, t2, t3, t4)
    sources = (x0, x1, x2, x3, x4)
    width = own.shape[1]
    here = pl.ds(pl.multiple_of(lax.axis_index("grp") * LANES, LANES), LANES)
    dual_column = dual[here, 0:1]
    mass = jnp.zeros((LANES, 1), jnp.float32)
    carried = jnp.zeros((LANES, width), jnp.float32)
    for p in range(WINDOW):
        bias = jnp.where(is_listed(mask, p), pot[p : p + 1, :], NEG)
        weight = jnp.exp2(dot_nt(mine[...], targets[p][...]) * TWO_KAPPA + (dual_column + bias))
        weight = weight.astype(jnp.bfloat16)
        mass = mass + jnp.sum(weight.astype(jnp.float32), axis=1, keepdims=True)
        carried = carried + jnp.dot(weight, targets[p][...], preferred_element_type=jnp.float32)
    source_out[...] = 2.0 * (mine[...].astype(jnp.float32) * mass - carried)

    bias = jnp.broadcast_to(pot[0:1, here], (LANES, LANES)).T[:, 0:1]
    lane = lax.broadcasted_iota(jnp.int32, (1, LANES), 1)
    mass = jnp.zeros((LANES, 1), jnp.float32)
    pulled = jnp.zeros((LANES, width), jnp.float32)
    for p in range(WINDOW):
        low, high = ((2, 2), (1, 3), (3, 1), (0, 0), (4, 4))[p]
        slot = jnp.where(is_even(), low, high)
        taken = jnp.max(jnp.where(lane == slot, around[p, 1:2, 0:LANES], 0.0), axis=1, keepdims=True)
        shift = jnp.where(taken > 0.5, around[p, 0:1, :], NEG) + bias
        weight = jnp.exp2(dot_nt(own[...], sources[p][...]) * TWO_KAPPA + shift)
        weight = weight.astype(jnp.bfloat16)
        mass = mass + jnp.sum(weight.astype(jnp.float32), axis=1, keepdims=True)
        pulled = pulled + jnp.dot(weight, sources[p][...], preferred_element_type=jnp.float32)
    target_out[...] = 2.0 * (own[...].astype(jnp.float32) * mass - pulled)


def gradients(mask, pot, dual, around, mine, own, targets, sources):
    width = mine.shape[1]
    count = sources[0].shape[0]
    part = jax.ShapeDtypeStruct((LANES, width), jnp.float32)
    pairs = 2 * WINDOW * count * LANES
    return pl.pallas_call(
        grad_kernel,
        out_shape=(part, part),
        in_specs=[SMEM] + [VMEM] * 15,
        out_specs=(VMEM, VMEM),
        compiler_params=pltpu.CompilerParams(vmem_limit_bytes=SCOPED),
        cost_estimate=pl.CostEstimate(
            flops=4 * pairs * width, bytes_accessed=20 * count * width, transcendentals=pairs
        ),
        name="plan_gradients",
    )(mask, pot, dual, around, mine, own, *targets, *sources)


def neighbours(block, even):
    above = shifted(block, -2)
    below = shifted(block, 2)
    mate = swap_mate(block)
    cross = swap_mate(jnp.where(even, above, below))
    return block, mate, cross, above, below


def shards(source, target, pair_mask):
    row = lax.axis_index("row")
    even = row % 2 == 0
    up = (row // 2) // (1 + row % 2) % 2 == 0
    targets = neighbours(gathered(target), even)
    rows = gathered(source)
    rows, even, up = lax.optimization_barrier((rows, even, up))
    entries, partial, top, base = first_step(pair_mask, rows, targets)
    total, (mate, above, below) = column_totals(
        partial,
        even,
        up,
        cargo=(rows,),
        movers=(swap_mate,),
        landed=(shifted(rows, -2), shifted(rows, 2)),
    )
    (partial,) = later_step(False, pair_mask, entries, -total, base, top, rows, targets)
    total, (cross,) = column_totals(
        partial,
        even,
        up,
        False,
        (above, below),
        (lambda a, b: swap_mate(jnp.where(even, a, b)),),
    )
    partial, dual = later_step(True, pair_mask, entries, -total, base, top, rows, targets)
    total, around = column_totals(partial, even, up, True)
    sources = (rows, mate, cross, above, below)
    return gradients(pair_mask, -total, dual, around, source, target, targets, sources)


def solution(mesh):
    placed = (P(("row", "grp"), None), P(("row", "grp"), None), P("row", None))
    return jax.shard_map(
        shards,
        mesh=mesh,
        in_specs=placed,
        out_specs=(P(("row", "grp"), None), P(("row", "grp"), None)),
        check_vma=False,
    )
```
